256 devices in a mesh: teacher: 4 (over y), group: 8 (over z_lo, core), dp: 8 (over x, z_hi).
Axes of the slice: x: 4, y: 4, z: 8 (z_hi: 2, z_lo: 4; z = z_hi * 4 + z_lo), core: 2. Of those that a mesh axis runs over, the one named last changes fastest.
Arguments:
- teacher_feats: bfloat16 [32, 256, 4096], P('teacher', ('group', 'dp')), may hold values from -6 to 6
- student_feats: bfloat16 [8, 4, 8, 2, 256, 768], P('group', 'teacher', 'dp'), may hold values from -6 to 6
- norm_gain: float32 [8, 768], P('group'), may hold values from 0.25 to 1.75
- head_weight: bfloat16 [8, 4096, 768], P('group', ('teacher', 'dp')), may hold values from -0.21875 to 0.21875
- slot_image: int32 [8, 4, 8, 2], P(None, 'teacher'), may hold values from 0 to 7, as said below
- slot_count: int32 [8, 4, 8], P(None, 'teacher'), may hold values from 0 to 2, as said below
Outputs:
- loss: float32 [8], P('group')
- student_grad: bfloat16 [8, 4, 8, 2, 256, 768], P('group', 'teacher', 'dp')
- head_grad: float32 [8, 4096, 768], P('group', ('teacher', 'dp'))
- gain_grad: float32 [8, 768], P('group')
The draws below stay inside these ranges and needn't reach their ends.
Inputs may be any that keep to these rules, and one draw needn't show every extreme that they name: `slot_count`: for each student and teacher batch, the counts of the 8 devices sum to 8; one device holds exactly 2 and another none. `slot_image`: for each student and teacher batch, the used slots of the devices in device order list each of the batch's 8 images once; unused slots hold image numbers to be ignored.
All inputs are finite; a program needn't handle non-finite values.
Results may differ from the reference program's by a relative error of at most 0.017.
Values may be sent and summed in bfloat16 or wider, within the bound.
A program may use at most 128 MiB of HBM per device.

```python
import jax
import jax.numpy as jnp
from jax import lax

FEAT = 4096
WIDTH = 768
PATCHES = 256
IMG_DP = 1
CAP = 2
IMG_T = 8
IMAGES = 32
STUDENTS = 8
N_TEACHER = 4
N_DP = 8


def slot_tables(key):
    keys = jax.random.split(key, STUDENTS * N_TEACHER)

    def single(subkey):
        key_busy, key_empty, key_order = jax.random.split(subkey, 3)
        busiest = jax.random.randint(key_busy, (), 0, N_DP)
        emptiest = (busiest + 1 + jax.random.randint(key_empty, (), 0, N_DP - 1)) % N_DP
        lane_index = jnp.arange(N_DP, dtype=jnp.int32)
        counts = jnp.where(lane_index == busiest, CAP, jnp.where(lane_index == emptiest, 0, IMG_DP)).astype(jnp.int32)
        ordering = jax.random.permutation(key_order, IMG_T).astype(jnp.int32)
        starts = jnp.cumsum(counts) - counts
        position = (starts[:, None] + jnp.arange(CAP, dtype=jnp.int32)[None, :]) % IMG_T
        return (ordering[position].astype(jnp.int32), counts)
    images, counts = jax.vmap(single)(keys)
    return (images.reshape(STUDENTS, N_TEACHER, N_DP, CAP), counts.reshape(STUDENTS, N_TEACHER, N_DP))


def draw_slot_image(key, part):
    return slot_tables(key)[0]


def draw_slot_count(key, part):
    return slot_tables(key)[1]


def levels(own_key, shape, cuts, low, top_value):
    factor_of, own = 1.0, jax.random.fold_in(own_key, 6)
    for dim, shards_of in cuts:
        draws = jnp.exp(jax.random.uniform(jax.random.fold_in(own, dim), (shards_of,), jnp.float32, low / len(cuts), top_value / len(cuts)))
        factor_of = factor_of * jnp.repeat(draws, shape[dim] // shards_of).reshape([-1 if axis == dim else 1 for axis in range(len(shape))])
    return factor_of


def normal_values(stream_key, dims, scale, most, shards=(), held_as=jnp.bfloat16):
    entries = scale * jax.random.normal(stream_key, dims, jnp.float32)
    if shards:
        entries = entries * levels(stream_key, dims, shards, -0.22, 0.18)
    return jnp.clip(entries, -most, most).astype(held_as)


def setup_inputs(seed: int = 0) -> dict:
    seeds = jax.random.split(jax.random.key(seed), 7)
    return {
        "teacher_feats": normal_values(seeds[0], (IMAGES, PATCHES, FEAT), 1.0, 6.0, ((0, 4), (1, 64))),
        "student_feats": normal_values(seeds[1], (STUDENTS, N_TEACHER, N_DP, CAP, PATCHES, WIDTH), 1.0, 6.0, ((0, 8), (1, 4), (2, 8))),
        "norm_gain": jnp.clip(1.0 + 0.15 * jax.random.normal(seeds[2], (STUDENTS, WIDTH), jnp.float32), 0.25, 1.75),
        "head_weight": normal_values(seeds[3], (STUDENTS, FEAT, WIDTH), WIDTH ** -0.5, 0.21875, ((0, 8), (1, 32))),
        "slot_image": draw_slot_image(jax.random.fold_in(seeds[6], 71), 0),
        "slot_count": draw_slot_count(jax.random.fold_in(seeds[6], 71), 0),
    }


def normalize(values, gain):
    center = values - lax.optimization_barrier(jnp.mean(values, axis=-1, keepdims=True))
    spread = lax.optimization_barrier(jnp.mean(center * center, axis=-1, keepdims=True))
    return center * lax.rsqrt(spread + 1e-06) * gain

def token_terms(logits, target, weight):
    target32 = target.astype(jnp.float32)
    inner_sum = lax.optimization_barrier(jnp.mean(logits * target32, axis=-1))
    logit_sq = lax.optimization_barrier(jnp.mean(logits * logits, axis=-1))
    target_sq = lax.optimization_barrier(jnp.mean(target32 * target32, axis=-1))
    cosine = inner_sum * lax.rsqrt(logit_sq + 1e-06) * lax.rsqrt(target_sq + 1e-06)
    return jnp.sum(weight * (1.0 - cosine))

def reference(teacher_feats, student_feats, norm_gain, head_weight, slot_image, slot_count):
    total = IMAGES * PATCHES
    scale = FEAT / 16.0
    device_rows = CAP * PATCHES

    def per_student(inputs):
        feats, gain, weights, images, counts = inputs
        index = (jnp.arange(N_TEACHER, dtype=jnp.int32)[:, None, None] * IMG_T + images).reshape(-1)
        target = teacher_feats[index].reshape(-1, FEAT)
        used = (jnp.arange(CAP, dtype=jnp.int32)[None, None, :] < counts[:, :, None]).astype(jnp.float32)
        weight = jnp.repeat(used.reshape(-1), PATCHES)
        values = feats.reshape(-1, WIDTH).astype(jnp.float32)
        normed, pullback = jax.vjp(normalize, values, gain)
        normed_b = normed.astype(jnp.bfloat16)
        logits = lax.dot_general(normed_b, weights, (((1,), (1,)), ((), ())), preferred_element_type=jnp.float32)
        loss_value = token_terms(logits, target, weight) / total
        dlogits = jax.grad(lambda inside: scale * token_terms(inside, target, weight))(logits).astype(jnp.bfloat16)
        dl_blocks = dlogits.reshape(N_TEACHER * N_DP, device_rows, FEAT)
        nb_blocks = normed_b.reshape(N_TEACHER * N_DP, device_rows, WIDTH)

        def add_part(accum, pair):
            part = lax.dot_general(pair[0], pair[1], (((0,), (0,)), ((), ())), preferred_element_type=jnp.float32)
            rounded = lax.optimization_barrier(part.astype(jnp.bfloat16))
            return (accum + rounded.astype(jnp.float32), None)
        grad_head, unused = lax.scan(add_part, jnp.zeros((FEAT, WIDTH), jnp.float32), (dl_blocks, nb_blocks))
        dnormed = jnp.dot(dlogits, weights, preferred_element_type=jnp.float32)
        grad_values, grad_gain = pullback(dnormed)
        return (loss_value, grad_values.astype(jnp.bfloat16).reshape(feats.shape), grad_head, grad_gain)
    results = lax.map(per_student, (student_feats, norm_gain, head_weight, slot_image, slot_count))
    return (results[0], results[1], results[2], results[3])
```

```python
import jax
import jax.numpy as jnp
from jax import lax
from jax.experimental import pallas as pl
from jax.experimental.pallas import tpu as pltpu
from jax.sharding import PartitionSpec as P

MESH = pl.DeviceIdType.MESH
F32 = jnp.float32
BF16 = jnp.bfloat16

FEAT = 4096
WIDTH = 768
PATCHES = 256
SLICE = 1024
MAIN = 256
EXT = 64
BLOCK = MAIN + EXT
ROWS = 4 * BLOCK
TOTAL = 32 * PATCHES
SEMS = 96


def permutation(size, source_of):
    rows = lax.broadcasted_iota(jnp.int32, (size, size), 0)
    cols = lax.broadcasted_iota(jnp.int32, (size, size), 1)
    return jnp.where(source_of(rows) == cols, 1.0, 0.0).astype(BF16)


def image_order(n):
    return (n // 4 % 4) * 32 + (n // 16) * 4 + n % 4


def patch_order(n):
    return (n // 32) * 32 + (n // 4 % 4) * 8 + (n // 16 % 2) * 4 + n % 4


def dot(a, b, dims):
    return lax.dot_general(a, b, (dims, ((), ())), preferred_element_type=F32)


def kernel(
    teach, feats, gain, head, info,
    small_o, sgrad_o, hgrad_o,
    arrived, target, heads, rows_b, extra_out, extra_in,
    xhat, rstd, logits, dlogits, sums, cols,
    stat_out, stat_in, tiny_out, tiny_in,
    g_out, g_own, g_in, gz_out, gz_in,
    d_out, d_own, d_in, e_out, e_in,
    send_sem, recv_sem,
):
    t = lax.axis_index("teacher")
    g = lax.axis_index("group")
    d = lax.axis_index("dp")
    x, zh = d // 2, d % 2
    zl, core = g // 2, g % 2
    z = zh * 4 + zl

    def device(dx=0, dy=0, dz=0, dc=0):
        to_z = (z + dz + 8) % 8
        return {
            "teacher": (t + dy + 4) % 4,
            "group": (to_z % 4) * 2 + (core + dc) % 2,
            "dp": ((x + dx + 4) % 4) * 2 + to_z // 4,
        }

    used = [0]
    copies = []

    def send(src, dst, to):
        index = used[0]
        used[0] += 1
        copy = pltpu.make_async_remote_copy(
            src_ref=src, dst_ref=dst, send_sem=send_sem.at[index], recv_sem=recv_sem.at[index],
            device_id=to, device_id_type=MESH,
        )
        copy.start()
        copies.append(copy)
        return copy

    barrier = pltpu.get_barrier_semaphore()
    partners = [device(dx=k) for k in (1, 2, 3)] + [device(dy=k) for k in (1, 2, 3)]
    partners += [device(dz=k) for k in (1, -1, 4)] + [device(dc=1)]
    for to in partners:
        pl.semaphore_signal(barrier, inc=1, device_id=to, device_id_type=MESH)
    pl.semaphore_wait(barrier, len(partners))

    mine = t * 2 + zh
    head_z = send(head, heads.at[mine], device(dz=4))
    slices = [send(teach.at[(x + k) % 4], arrived.at[x], device(dx=k)) for k in (1, 3, 2)]
    head_y = [send(head, heads.at[mine], device(dy=k)) for k in (1, 3, 2)]
    heads[mine] = head[...]
    arrived[x] = teach[x]

    count = info[128 + g * 8 + d]
    second = jnp.where(count >= 2, 1.0, 0.0).astype(F32)
    order = permutation(MAIN, patch_order)
    base = pl.multiple_of(x * BLOCK, BLOCK)
    for slot in range(2):
        part = pl.ds(slot * MAIN, MAIN)
        values = dot(order, feats[part, :], ((1,), (0,)))
        center = values - jnp.mean(values, axis=-1, keepdims=True)
        rs = lax.rsqrt(jnp.mean(center * center, axis=-1, keepdims=True) + 1e-06)
        unit = center * rs
        xhat[part, :] = unit
        rstd[part, :] = jnp.broadcast_to(rs, (MAIN, 128))
        normed = unit * gain[...]
        if slot == 0:
            rows_b[pl.ds(base, MAIN), :] = normed.astype(BF16)
            here = rows_b.at[pl.ds(base, MAIN), :]
            ring = [send(here, here, device(dx=k)) for k in (1, -1)]
        else:
            extra_out[...] = (normed * second).astype(BF16)
    parts = [
        send(
            extra_out.at[pl.ds(pl.multiple_of((x + k) % 4 * EXT, EXT), EXT), :],
            extra_in.at[k - 1], device(dx=k),
        )
        for k in (1, 3, 2)
    ]

    for copy in slices:
        copy.wait_recv()
    own = dot(permutation(128, image_order), arrived[...].reshape(128, SLICE), ((1,), (0,)))
    block = zl * 4 + core * 2 + zh
    target[:, block] = own.astype(BF16).reshape(8, 16, SLICE)

    def chunk(step, half):
        at = (z + step + 8) % 8
        return target.at[pl.ds(half * 4, 4), (at % 4) * 4 + core * 2 + at // 4]

    shared = []

    def pass_on(step, half, ways):
        piece = chunk(step, half)
        found = [send(piece, piece, device(dz=way)) for way in ways]
        shared.append(send(piece, piece, device(dc=1)))
        return found

    first = [pass_on(0, half, (1, -1)) for half in range(2)]
    from_low = [first[0][0], first[1][0]]
    from_high = [first[0][1], first[1][1]]

    head_z.wait_recv()
    theirs = t * 2 + 1 - zh
    there = heads.at[theirs]
    head_y += [send(there, there, device(dy=k)) for k in (1, 3, 2)]

    for copy in parts:
        copy.wait_recv()
    mine_q = extra_out[pl.ds(pl.multiple_of(x * EXT, EXT), EXT), :].astype(F32)
    mine_q += extra_in[0].astype(F32) + extra_in[1].astype(F32) + extra_in[2].astype(F32)
    rows_b[pl.ds(base + MAIN, EXT), :] = mine_q.astype(BF16)
    tail = rows_b.at[pl.ds(base + MAIN, EXT), :]
    tails = [send(tail, tail, device(dx=k)) for k in (1, 3, 2)]

    def ring_step(step):
        last = step == 3
        for half in range(2):
            from_low[half].wait_recv()
            ways = () if last and half == 1 else (1,)
            found = pass_on(-step, half, ways)
            from_low[half] = found[0] if found else None
            from_high[half].wait_recv()
            ways = () if last and half == 0 else (-1,)
            found = pass_on(step, half, ways)
            from_high[half] = found[0] if found else None

    ring_step(1)

    for copy in ring:
        copy.wait_recv()
    left = rows_b.at[pl.ds(pl.multiple_of((x + 3) % 4 * BLOCK, BLOCK), MAIN // 2), :]
    right = rows_b.at[pl.ds((x + 1) % 4 * BLOCK + MAIN // 2, MAIN // 2), :]
    ring = [send(left, left, device(dx=1)), send(right, right, device(dx=-1))]

    ring_step(2)
    for copy in head_y:
        copy.wait_recv()
    ring_step(3)
    for copy in ring + tails:
        copy.wait_recv()

    def forward(b, carry):
        at = pl.ds(pl.multiple_of(b * BLOCK, BLOCK), BLOCK)
        logits[at, :] = dot(rows_b[at, :], heads[...].reshape(SLICE, WIDTH), ((1,), (1,)))
        return carry

    lax.fori_loop(0, 4, forward, 0)

    from_low[0].wait_recv()
    pass_on(-4, 0, ())
    from_high[1].wait_recv()
    pass_on(4, 1, ())
    for copy in shared:
        copy.wait_recv()

    counts = [info[128 + g * 8 + b * 2 + zh] for b in range(4)]
    extra_image = jnp.int32(0)
    extra_weight = jnp.float32(0)
    main_weight = []
    for b in range(4):
        twice = counts[b] >= 2
        extra_image += jnp.where(twice, info[g * 16 + b * 4 + zh * 2 + 1], 0)
        extra_weight += jnp.where(twice, 1.0, 0.0).astype(F32)
        main_weight.append(jnp.where(counts[b] >= 1, 1.0, 0.0).astype(F32))

    def targets(b):
        image = info[g * 16 + b * 4 + zh * 2]
        main = target[image].reshape(MAIN, SLICE)
        ext = target[extra_image, pl.ds(b * 4, 4)].reshape(EXT, SLICE)
        return jnp.concatenate([main, ext], axis=0).astype(F32)

    lane = lax.broadcasted_iota(jnp.int32, (BLOCK, 128), 1)

    def statistics(b, carry):
        at = pl.ds(pl.multiple_of(b * BLOCK, BLOCK), BLOCK)
        lg = logits[at, :]
        tg = targets(b)
        inner = jnp.sum(lg * tg, axis=-1, keepdims=True)
        lsq = jnp.sum(lg * lg, axis=-1, keepdims=True)
        tsq = jnp.sum(tg * tg, axis=-1, keepdims=True)
        sums[at, :] = jnp.where(lane == 0, inner, jnp.where(lane == 1, lsq, tsq))
        return carry

    lax.fori_loop(0, 4, statistics, 0)
    for k in range(ROWS // 128):
        stat_out[:, k * 128:(k + 1) * 128] = jnp.transpose(sums[k * 128:(k + 1) * 128, :])[:8]
    stats = [send(stat_out, stat_in.at[k - 1], device(dx=k)) for k in (1, 3, 2)]
    for copy in stats:
        copy.wait_recv()
    total = (stat_out[...] + stat_in[0] + stat_in[1] + stat_in[2]) * (1.0 / FEAT)
    inner, lsq, tsq = total[0:1], total[1:2], total[2:3]
    rl, rt = lax.rsqrt(lsq + 1e-06), lax.rsqrt(tsq + 1e-06)
    row = lax.broadcasted_iota(jnp.int32, (1, ROWS), 1)
    weight = jnp.zeros((1, ROWS), F32)
    for b in range(4):
        low = b * BLOCK
        weight = jnp.where((row >= low) & (row < low + MAIN), main_weight[b], weight)
        weight = jnp.where((row >= low + MAIN) & (row < low + BLOCK), extra_weight, weight)
    here = (row >= x * BLOCK) & (row < x * BLOCK + BLOCK)
    loss = jnp.sum(jnp.where(here, weight * (1.0 - inner * rl * rt), 0.0)) * (1.0 / TOTAL)
    on_target = weight * rl * rt * (-1.0 / 16.0)
    on_logits = weight * inner * rt * rl * rl * rl * (1.0 / 16.0)
    pair = jnp.concatenate([on_target, on_logits, jnp.zeros((126, ROWS), F32)], axis=0)
    for k in range(ROWS // 128):
        cols[k * 128:(k + 1) * 128, :] = jnp.transpose(pair[:, k * 128:(k + 1) * 128])

    def backward(b, carry):
        at = pl.ds(pl.multiple_of(b * BLOCK, BLOCK), BLOCK)
        factors = cols[at, :]
        dl = factors[:, 0:1] * targets(b) + factors[:, 1:2] * logits[at, :]
        dlogits[at, :] = dl.astype(BF16)
        return carry

    lax.fori_loop(0, 4, backward, 0)

    gain_part = jnp.zeros((1, WIDTH), F32)
    away, near = [], []
    far = pl.ds(pl.multiple_of((1 - zh) * 128, 128), 128)
    close = pl.ds(pl.multiple_of(zh * 128, 128), 128)
    for k in (2, 1, 3, 0):
        to = (t + k) % 4
        columns = pl.ds(pl.multiple_of(to * 256, 256), 256)
        part = dot(dlogits[:, columns], rows_b[...], ((0,), (0,)))
        weights = heads[pl.ds(to * 2, 2)].reshape(256, WIDTH).astype(F32)
        gain_part += jnp.sum(part * weights, axis=0, keepdims=True)
        if k:
            g_out[k - 1] = part.astype(BF16)
            away.append(send(g_out.at[k - 1, far], g_in.at[0, k - 1], device(dy=k)))
        else:
            g_own[...] = part
    for k in (2, 1, 3):
        near.append(send(g_out.at[k - 1, close], g_in.at[1, k - 1], device(dy=k)))

    which = lax.broadcasted_iota(jnp.int32, (8, WIDTH), 0)
    tiny = jnp.where(which == 0, gain_part / gain[...], jnp.where(which == 1, loss, 0.0))
    tiny_out[0] = tiny
    tiny_x = [send(tiny_out.at[0], tiny_in.at[k - 1], device(dx=k)) for k in (1, 3, 2)]

    ext_parts, main_parts = [], []
    for k in (2, 1, 3, 0):
        at = pl.ds(pl.multiple_of((x + k) % 4 * BLOCK, BLOCK), BLOCK)
        part = dot(dlogits[at, :], heads[...].reshape(SLICE, WIDTH), ((1,), (0,)))
        if k:
            d_out[k - 1] = part.astype(BF16)
            rest = pl.ds(MAIN, EXT)
            ext_parts.append(send(d_out.at[k - 1, rest], d_in.at[k - 1, rest], device(dx=k)))
        else:
            d_own[...] = part
    for k in (2, 1, 3):
        rest = pl.ds(0, MAIN)
        main_parts.append(send(d_out.at[k - 1, rest], d_in.at[k - 1, rest], device(dx=k)))

    for copy in tiny_x:
        copy.wait_recv()
    tiny += tiny_in[0] + tiny_in[1] + tiny_in[2]
    tiny_out[1] = tiny
    tiny_y = [send(tiny_out.at[1], tiny_in.at[2 + k], device(dy=k)) for k in (1, 3, 2)]

    for copy in ext_parts:
        copy.wait_recv()
    rest = pl.ds(MAIN, EXT)
    ext_sum = d_own[rest, :]
    for k in range(3):
        ext_sum += d_in[k, rest].astype(F32)
    e_out[...] = ext_sum.astype(BF16)
    ext_all = [send(e_out, e_in.at[k - 1], device(dx=k)) for k in (1, 3, 2)]

    for copy in away:
        copy.wait_recv()
    part = g_own[far, :]
    for k in range(3):
        part += g_in[0, k].astype(F32)
    gz_out[...] = part.astype(BF16)
    across = send(gz_out, gz_in, device(dz=4))

    for copy in tiny_y:
        copy.wait_recv()
    tiny += tiny_in[3] + tiny_in[4] + tiny_in[5]
    tiny_out[2] = tiny
    tiny_z = send(tiny_out.at[2], tiny_in.at[6], device(dz=4))

    def finish(dnormed, part):
        dx = dnormed * gain[...]
        unit = xhat[part, :]
        drop = jnp.mean(dx, axis=-1, keepdims=True)
        along = jnp.mean(dx * unit, axis=-1, keepdims=True)
        out = (rstd[part, :][:, 0:1] * (dx - drop - unit * along)).astype(BF16)
        sgrad_o[part, :] = dot(order, out, ((0,), (0,))).astype(BF16)

    for copy in ext_all:
        copy.wait_recv()
    quarters = []
    for q in range(4):
        got = jnp.where(x == q, ext_sum, 0.0)
        for k in (1, 2, 3):
            got = jnp.where((x + 4 - k) % 4 == q, e_in[k - 1].astype(F32), got)
        quarters.append(got * second)
    finish(jnp.concatenate(quarters, axis=0), pl.ds(MAIN, MAIN))

    for copy in main_parts:
        copy.wait_recv()
    rest = pl.ds(0, MAIN)
    dn = d_own[rest, :]
    for k in range(3):
        dn += d_in[k, rest].astype(F32)
    finish(dn, rest)

    for copy in near:
        copy.wait_recv()
    part = g_own[close, :]
    for k in range(3):
        part += g_in[1, k].astype(F32)
    across.wait_recv()
    hgrad_o[...] = part + gz_in[...].astype(F32)
    tiny_z.wait_recv()
    small_o[...] = tiny + tiny_in[6]
    for copy in copies:
        copy.wait_send()


def shards(teacher_feats, student_feats, norm_gain, head_weight, slot_image, slot_count):
    by_slice = teacher_feats.reshape(32, 4, 4, 256).transpose(2, 0, 1, 3).reshape(4, 32, SLICE)
    info = jnp.concatenate([slot_image.reshape(-1), slot_count.reshape(-1)])
    vmem = pl.BlockSpec(memory_space=pltpu.VMEM)
    smem = pl.BlockSpec(memory_space=pltpu.SMEM)
    small, sgrad, hgrad = pl.pallas_call(
        kernel,
        out_shape=(
            jax.ShapeDtypeStruct((8, WIDTH), F32),
            jax.ShapeDtypeStruct((2 * MAIN, WIDTH), BF16),
            jax.ShapeDtypeStruct((128, WIDTH), F32),
        ),
        in_specs=[vmem, vmem, vmem, vmem, smem],
        out_specs=(vmem, vmem, vmem),
        scratch_shapes=[
            pltpu.VMEM((4, 32, SLICE), BF16),
            pltpu.VMEM((8, 16, 16, SLICE), BF16),
            pltpu.VMEM((8, 128, WIDTH), BF16),
            pltpu.VMEM((ROWS, WIDTH), BF16),
            pltpu.VMEM((MAIN, WIDTH), BF16),
            pltpu.VMEM((3, EXT, WIDTH), BF16),
            pltpu.VMEM((2 * MAIN, WIDTH), F32),
            pltpu.VMEM((2 * MAIN, 128), F32),
            pltpu.VMEM((ROWS, SLICE), F32),
            pltpu.VMEM((ROWS, SLICE), BF16),
            pltpu.VMEM((ROWS, 128), F32),
            pltpu.VMEM((ROWS, 128), F32),
            pltpu.VMEM((8, ROWS), F32),
            pltpu.VMEM((3, 8, ROWS), F32),
            pltpu.VMEM((3, 8, WIDTH), F32),
            pltpu.VMEM((7, 8, WIDTH), F32),
            pltpu.VMEM((3, 256, WIDTH), BF16),
            pltpu.VMEM((256, WIDTH), F32),
            pltpu.VMEM((2, 3, 128, WIDTH), BF16),
            pltpu.VMEM((128, WIDTH), BF16),
            pltpu.VMEM((128, WIDTH), BF16),
            pltpu.VMEM((3, BLOCK, WIDTH), BF16),
            pltpu.VMEM((BLOCK, WIDTH), F32),
            pltpu.VMEM((3, BLOCK, WIDTH), BF16),
            pltpu.VMEM((EXT, WIDTH), BF16),
            pltpu.VMEM((3, EXT, WIDTH), BF16),
            pltpu.SemaphoreType.DMA((SEMS,)),
            pltpu.SemaphoreType.DMA((SEMS,)),
        ],
        compiler_params=pltpu.CompilerParams(
            collective_id=0, has_side_effects=True, vmem_limit_bytes=56 << 20
        ),
        name="head_step",
    )(by_slice, student_feats.reshape(2 * MAIN, WIDTH), norm_gain, head_weight.reshape(128, WIDTH), info)
    return (
        small[1, 0:1],
        sgrad.reshape(student_feats.shape),
        hgrad.reshape(1, 128, WIDTH),
        small[0:1],
    )


def solution(mesh):
    return jax.shard_map(
        shards,
        mesh=mesh,
        in_specs=(
            P("teacher", ("group", "dp"), None),
            P("group", "teacher", "dp", None, None, None),
            P("group", None),
            P("group", ("teacher", "dp"), None),
            P(None, "teacher", None, None),
            P(None, "teacher", None),
        ),
        out_specs=(
            P("group"),
            P("group", "teacher", "dp", None, None, None),
            P("group", ("teacher", "dp"), None),
            P("group", None),
        ),
        check_vma=False,
    )
```

```python
import jax
import jax.numpy as jnp
from jax import lax
from jax.experimental import pallas as pl
from jax.experimental.pallas import tpu as pltpu
from jax.sharding import PartitionSpec as P

MESH = pl.DeviceIdType.MESH
F32 = jnp.float32
BF16 = jnp.bfloat16

FEAT = 4096
WIDTH = 768
PATCHES = 256
SLICE = 1024
MAIN = 256
PART = 32
GROUP = 640
TOTAL = 32 * PATCHES
SEMS = 104


def permutation(size, source_of):
    rows = lax.broadcasted_iota(jnp.int32, (size, size), 0)
    cols = lax.broadcasted_iota(jnp.int32, (size, size), 1)
    return jnp.where(source_of(rows) == cols, 1.0, 0.0).astype(BF16)


def image_order(n):
    return (n // 4 % 4) * 32 + (n // 16) * 4 + n % 4


def dot(a, b, dims):
    return lax.dot_general(a, b, (dims, ((), ())), preferred_element_type=F32)


def kernel(
    teach, feats, gain, head, images, used_slots,
    loss_o, gain_o, sgrad_o, hgrad_o,
    arrived, near_target, far_target, heads, rows_b, extra_out, extra_in,
    xhat, rstd, logits, dlogits, sums, cols,
    stat_out, stat_in, tiny_out, tiny_in,
    g_out, g_own, g_in, gz_out, gz_in,
    d_all, d_out, d_in, e_in, e_all,
    feats_v, send_sem, recv_sem, local_sem,
):
    t = lax.axis_index("teacher")
    g = lax.axis_index("group")
    d = lax.axis_index("dp")
    x, zh = d // 2, d % 2
    zl, core = g // 2, g % 2
    z = zh * 4 + zl

    def device(dx=0, dy=0, dz=0, dc=0):
        to_z = (z + dz + 8) % 8
        return {
            "teacher": (t + dy + 4) % 4,
            "group": (to_z % 4) * 2 + (core + dc) % 2,
            "dp": ((x + dx + 4) % 4) * 2 + to_z // 4,
        }

    used = [0]
    copies = []

    def send(src, dst, to):
        index = used[0]
        used[0] += 1
        copy = pltpu.make_async_remote_copy(
            src_ref=src, dst_ref=dst, send_sem=send_sem.at[index], recv_sem=recv_sem.at[index],
            device_id=to, device_id_type=MESH,
        )
        copy.start()
        copies.append(copy)
        return copy

    def arrive(found):
        for copy in found:
            copy.wait_recv()

    barrier = pltpu.get_barrier_semaphore()
    partners = [device(dx=k) for k in (1, 2, 3)] + [device(dy=k) for k in (1, 2, 3)]
    partners += [device(dz=k) for k in (1, -1, 4)] + [device(dc=1)]
    for to in partners:
        pl.semaphore_signal(barrier, inc=1, device_id=to, device_id_type=MESH)

    def patch_order(n):
        h, q, c, xs, p = n // 128, n // 32 % 4, n // 16 % 2, n // 4 % 4, n % 4
        away = jnp.where(q == 1, 7, jnp.where(q == 2, 1, jnp.where(q == 3, 6, 0)))
        at = (z + away + 4 * h) % 8
        return (at % 4) * 64 + c * 32 + xs * 8 + (at // 4) * 4 + p

    mine = t * 2 + zh
    feats_in = pltpu.make_async_copy(feats, feats_v, local_sem.at[0])
    feats_in.start()

    def columns_of(to, b):
        return pl.ds(pl.multiple_of(b * SLICE + to * 256, 256), 256)

    owned = [pltpu.make_async_copy(head, heads.at[mine], local_sem.at[1])]
    for b in range(4):
        owned.append(pltpu.make_async_copy(
            teach.at[:, columns_of(x, b)], arrived.at[x, :, pl.ds(b * 256, 256)], local_sem.at[2 + b]
        ))
    for copy in owned:
        copy.start()
    feats_in.wait()
    second = jnp.where(used_slots[g, 0, d] >= 2, 1.0, 0.0).astype(F32)
    order = permutation(MAIN, patch_order)
    for slot in range(2):
        part = pl.ds(slot * MAIN, MAIN)
        values = dot(order, feats_v[part, :], ((1,), (0,)))
        center = values - jnp.mean(values, axis=-1, keepdims=True)
        rs = lax.rsqrt(jnp.mean(center * center, axis=-1, keepdims=True) + 1e-06)
        unit = center * rs
        xhat[part, :] = unit
        rstd[part, :] = jnp.broadcast_to(rs, (MAIN, 128))
        normed = unit * gain[...]
        if slot == 0:
            rows_b[:, :, x] = normed.astype(BF16).reshape(2, 4, PART, WIDTH)
        else:
            extra_out[...] = (normed * second).astype(BF16).reshape(2, 4, PART, WIDTH)
    pl.semaphore_wait(barrier, len(partners))

    slices = []
    for k in (1, 3, 2):
        for b in range(4):
            columns = columns_of((x + k) % 4, b)
            slices.append(send(teach.at[:, columns], arrived.at[x, :, pl.ds(b * 256, 256)], device(dx=k)))
    head_z = send(head, heads.at[mine], device(dz=4))
    parts = [send(extra_out.at[:, (x + k) % 4], extra_in.at[k - 1], device(dx=k)) for k in (1, 3, 2)]
    here = rows_b.at[:, :, x]
    ring = [send(here, here, device(dx=k)) for k in (1, -1)]
    head_y = [send(head, heads.at[mine], device(dy=k)) for k in (1, 3, 2)]

    arrive(slices)
    for copy in owned:
        copy.wait()
    own = dot(permutation(128, image_order), arrived[...].reshape(128, SLICE), ((1,), (0,)))
    target = (near_target, far_target)
    near_target[0, :, core] = own.astype(BF16).reshape(8, 16, SLICE)
    places = {0: (0, 0), -1: (0, 1), 1: (0, 2), -2: (0, 3), 4: (1, 0), -4: (1, 0), 3: (1, 1), -3: (1, 2), 2: (1, 3)}

    def chunk(step, half):
        h, q = places[step]
        return target[h].at[q, pl.ds(half * 4, 4), core]

    shared = [[], []]

    def pass_on(step, half, ways):
        piece = chunk(step, half)
        found = [send(piece, chunk(step - way, half), device(dz=way)) for way in ways]
        shared[places[step][0]].append(send(piece, piece, device(dc=1)))
        return found

    first = [pass_on(0, half, (1, -1)) for half in range(2)]
    from_low = [first[0][0], first[1][0]]
    from_high = [first[0][1], first[1][1]]

    def ring_step(step):
        last = step == 3
        for half in range(2):
            from_low[half].wait_recv()
            ways = () if last and half == 1 else (1,)
            found = pass_on(-step, half, ways)
            from_low[half] = found[0] if found else None
            from_high[half].wait_recv()
            ways = () if last and half == 0 else (-1,)
            found = pass_on(step, half, ways)
            from_high[half] = found[0] if found else None

    arrive(parts)
    quarter = extra_out[:, x].astype(F32)
    quarter += extra_in[0].astype(F32) + extra_in[1].astype(F32) + extra_in[2].astype(F32)
    rows_b[:, x, 4] = quarter.astype(BF16)
    tail = rows_b.at[:, x, 4]
    tails = [send(tail, tail, device(dx=k)) for k in (1, 3, 2)]

    head_z.wait_recv()
    theirs = heads.at[t * 2 + 1 - zh]
    head_y += [send(theirs, theirs, device(dy=k)) for k in (1, 3, 2)]

    ring_step(1)

    arrive(ring)
    left, right = rows_b.at[0, :, (x + 3) % 4], rows_b.at[1, :, (x + 1) % 4]
    ring = [send(left, left, device(dx=1)), send(right, right, device(dx=-1))]
    ring_step(2)
    ring_step(3)
    arrive(head_y)
    arrive(ring)
    arrive(tails)

    extra_image = jnp.int32(0)
    extra_weight = jnp.float32(0)
    image, weights = [], []
    for b in range(4):
        count = used_slots[g, 0, b * 2 + zh]
        twice = count >= 2
        extra_image += jnp.where(twice, images[g, 0, 1, b * 2 + zh], 0)
        extra_weight += jnp.where(twice, 1.0, 0.0).astype(F32)
        image.append(images[g, 0, 0, b * 2 + zh])
        weights.append(jnp.where(count >= 1, 1.0, 0.0).astype(F32))
    image.append(extra_image)
    weights.append(extra_weight)
    row = lax.broadcasted_iota(jnp.int32, (1, GROUP), 1)
    slot_of = (row // PART) % 5
    weight = jnp.zeros((1, GROUP), F32)
    for i in range(5):
        weight = jnp.where(slot_of == i, weights[i], weight)
    here = (slot_of == x) | ((slot_of == 4) & (row // 160 == x))
    loss = jnp.float32(0)

    def targets(h, q):
        found = [target[h][q, image[i]].reshape(PART, SLICE) for i in range(5)]
        return jnp.concatenate(found, axis=0).astype(F32)

    def forward(h):
        def step(b, carry):
            rows = rows_b[h, pl.ds(b * 2, 2)].reshape(320, WIDTH)
            out = dot(rows, heads[...].reshape(SLICE, WIDTH), ((1,), (1,)))
            logits[h, pl.ds(b * 2, 2)] = out.reshape(2, 160, SLICE)
            return carry

        lax.fori_loop(0, 2, step, 0)

    lane = lax.broadcasted_iota(jnp.int32, (160, 128), 1)

    def statistics(h):
        def step(q, carry):
            lg = logits[h, q]
            tg = targets(h, q)
            inner = jnp.sum(lg * tg, axis=-1, keepdims=True)
            lsq = jnp.sum(lg * lg, axis=-1, keepdims=True)
            tsq = jnp.sum(tg * tg, axis=-1, keepdims=True)
            at = pl.ds(pl.multiple_of(q * 160, 32), 160)
            sums[h, at, :] = jnp.where(lane == 0, inner, jnp.where(lane == 1, lsq, tsq))
            return carry

        lax.fori_loop(0, 4, step, 0)
        for k in range(GROUP // 128):
            at = pl.ds(k * 128, 128)
            stat_out[h, :, at] = jnp.transpose(sums[h, at, :])[:8]
        return [send(stat_out.at[h], stat_in.at[k - 1, h], device(dx=k)) for k in (1, 3, 2)]

    def factors(h):
        total = (stat_out[h] + stat_in[0, h] + stat_in[1, h] + stat_in[2, h]) * (1.0 / FEAT)
        inner, lsq, tsq = total[0:1], total[1:2], total[2:3]
        rl, rt = lax.rsqrt(lsq + 1e-06), lax.rsqrt(tsq + 1e-06)
        on_target = weight * rl * rt * (-1.0 / 16.0)
        on_logits = weight * inner * rt * rl * rl * rl * (1.0 / 16.0)
        pair = jnp.concatenate([on_target, on_logits, jnp.zeros((126, GROUP), F32)], axis=0)
        for k in range(GROUP // 128):
            cols[h, k * 128:(k + 1) * 128, :] = jnp.transpose(pair[:, k * 128:(k + 1) * 128])

        def step(q, carry):
            found = cols[h, pl.ds(pl.multiple_of(q * 160, 32), 160), :]
            dl = found[:, 0:1] * targets(h, q) + found[:, 1:2] * logits[h, q]
            dlogits[h, q] = dl.astype(BF16)
            return carry

        lax.fori_loop(0, 4, step, 0)
        return jnp.sum(jnp.where(here, weight * (1.0 - inner * rl * rt), 0.0)) * (1.0 / TOTAL)

    def row_gradient(h):
        def step(b, carry):
            part = dot(dlogits[h, pl.ds(b * 2, 2)].reshape(320, SLICE), heads[...].reshape(SLICE, WIDTH), ((1,), (0,)))
            part = part.reshape(2, 5, PART, WIDTH)
            d_all[h, pl.ds(b * 2, 2)] = part
            d_out[h, pl.ds(b * 2, 2)] = part.astype(BF16)
            return carry

        lax.fori_loop(0, 2, step, 0)
        ext = [send(d_out.at[h, (x + k) % 4, 4], e_in.at[k - 1, h], device(dx=k)) for k in (1, 3, 2)]
        main = [send(d_out.at[h, :, (x + k) % 4], d_in.at[k - 1, h], device(dx=k)) for k in (1, 3, 2)]
        return ext, main

    def extra_sum(h):
        total = d_all[h, x, 4]
        for k in range(3):
            total += e_in[k, h].astype(F32)
        e_all[h, x] = total.astype(BF16)
        piece = e_all.at[h, x]
        return [send(piece, piece, device(dx=k)) for k in (1, 3, 2)]

    forward(0)
    arrive(shared[0])
    stats_a = statistics(0)
    forward(1)
    from_low[0].wait_recv()
    pass_on(-4, 0, ())
    from_high[1].wait_recv()
    pass_on(4, 1, ())
    arrive(shared[1])
    stats_b = statistics(1)
    arrive(stats_a)
    loss += factors(0)
    ext_a, main_a = row_gradient(0)
    arrive(stats_b)
    loss += factors(1)

    gain_part = jnp.zeros((1, WIDTH), F32)
    away, near = [], []
    far = pl.ds(pl.multiple_of((1 - zh) * 128, 128), 128)
    close = pl.ds(pl.multiple_of(zh * 128, 128), 128)
    for k in (2, 1, 3, 0):
        to = (t + k) % 4
        columns = pl.ds(pl.multiple_of(to * 256, 256), 256)
        part = dot(
            dlogits[:, :, :, columns].reshape(2 * GROUP, 256), rows_b[...].reshape(2 * GROUP, WIDTH), ((0,), (0,))
        )
        head_part = heads[pl.ds(to * 2, 2)].reshape(256, WIDTH).astype(F32)
        gain_part += jnp.sum(part * head_part, axis=0, keepdims=True)
        if k:
            g_out[k - 1] = part.astype(BF16)
            away.append(send(g_out.at[k - 1, far], g_in.at[0, k - 1], device(dy=k)))
        else:
            g_own[...] = part
    for k in (2, 1, 3):
        near.append(send(g_out.at[k - 1, close], g_in.at[1, k - 1], device(dy=k)))

    which = lax.broadcasted_iota(jnp.int32, (8, WIDTH), 0)
    tiny = jnp.where(which == 0, gain_part / gain[...], jnp.where(which == 1, loss, 0.0))
    tiny_out[0] = tiny
    tiny_x = [send(tiny_out.at[0], tiny_in.at[k - 1], device(dx=k)) for k in (1, 3, 2)]

    ext_b, main_b = row_gradient(1)

    arrive(tiny_x)
    tiny += tiny_in[0] + tiny_in[1] + tiny_in[2]
    tiny_out[1] = tiny
    tiny_z = send(tiny_out.at[1], tiny_in.at[6], device(dz=4))

    arrive(ext_a)
    ext_all = extra_sum(0)
    arrive(ext_b)
    ext_all += extra_sum(1)

    tiny_z.wait_recv()
    tiny += tiny_in[6]
    tiny_out[2] = tiny
    tiny_y = [send(tiny_out.at[2], tiny_in.at[2 + k], device(dy=k)) for k in (1, 3, 2)]

    arrive(away)
    part = g_own[far, :]
    for k in range(3):
        part += g_in[0, k].astype(F32)
    gz_out[...] = part.astype(BF16)
    across = send(gz_out, gz_in, device(dz=4))

    def finish(dnormed, part):
        dx = dnormed.reshape(MAIN, WIDTH) * gain[...]
        unit = xhat[part, :]
        drop = jnp.mean(dx, axis=-1, keepdims=True)
        along = jnp.mean(dx * unit, axis=-1, keepdims=True)
        out = (rstd[part, :][:, 0:1] * (dx - drop - unit * along)).astype(BF16)
        sgrad_o[part, :] = dot(order, out, ((0,), (0,))).astype(BF16)

    arrive(ext_all)
    finish(e_all[...].astype(F32) * second, pl.ds(MAIN, MAIN))

    arrive(main_a)
    arrive(main_b)
    dn = d_all[:, :, x]
    for k in range(3):
        dn += d_in[k].astype(F32)
    finish(dn, pl.ds(0, MAIN))

    arrive(near)
    part = g_own[close, :]
    for k in range(3):
        part += g_in[1, k].astype(F32)
    across.wait_recv()
    hgrad_o[...] = part + gz_in[...].astype(F32)
    arrive(tiny_y)
    tiny += tiny_in[3] + tiny_in[4] + tiny_in[5]
    gain_o[...] = tiny[0:1]
    loss_o[0] = tiny[1, 0]
    for copy in copies:
        copy.wait_send()


def shards(teacher_feats, student_feats, norm_gain, head_weight, slot_image, slot_count):
    vmem = pl.BlockSpec(memory_space=pltpu.VMEM)
    smem = pl.BlockSpec(memory_space=pltpu.SMEM)
    anywhere = pl.BlockSpec(memory_space=pl.ANY)
    loss, gain_grad, sgrad, hgrad = pl.pallas_call(
        kernel,
        out_shape=(
            jax.ShapeDtypeStruct((1,), F32),
            jax.ShapeDtypeStruct((1, WIDTH), F32),
            pltpu.VMEM((2 * MAIN, WIDTH), BF16),
            pltpu.VMEM((128, WIDTH), F32),
        ),
        in_specs=[anywhere, anywhere, vmem, anywhere, smem, smem],
        out_specs=(smem, vmem, vmem, vmem),
        scratch_shapes=[
            pltpu.VMEM((4, 32, SLICE), BF16),
            pltpu.VMEM((4, 8, 2, 16, SLICE), BF16),
            pltpu.VMEM((4, 8, 2, 16, SLICE), BF16),
            pltpu.VMEM((8, 128, WIDTH), BF16),
            pltpu.VMEM((2, 4, 5, PART, WIDTH), BF16),
            pltpu.VMEM((2, 4, PART, WIDTH), BF16),
            pltpu.VMEM((3, 2, PART, WIDTH), BF16),
            pltpu.VMEM((2 * MAIN, WIDTH), F32),
            pltpu.VMEM((2 * MAIN, 128), F32),
            pltpu.VMEM((2, 4, 160, SLICE), F32),
            pltpu.VMEM((2, 4, 160, SLICE), BF16),
            pltpu.VMEM((2, GROUP, 128), F32),
            pltpu.VMEM((2, GROUP, 128), F32),
            pltpu.VMEM((2, 8, GROUP), F32),
            pltpu.VMEM((3, 2, 8, GROUP), F32),
            pltpu.VMEM((3, 8, WIDTH), F32),
            pltpu.VMEM((7, 8, WIDTH), F32),
            pltpu.VMEM((3, 256, WIDTH), BF16),
            pltpu.VMEM((256, WIDTH), F32),
            pltpu.VMEM((2, 3, 128, WIDTH), BF16),
            pltpu.VMEM((128, WIDTH), BF16),
            pltpu.VMEM((128, WIDTH), BF16),
            pltpu.VMEM((2, 4, 5, PART, WIDTH), F32),
            pltpu.VMEM((2, 4, 5, PART, WIDTH), BF16),
            pltpu.VMEM((3, 2, 4, PART, WIDTH), BF16),
            pltpu.VMEM((3, 2, PART, WIDTH), BF16),
            pltpu.VMEM((2, 4, PART, WIDTH), BF16),
            pltpu.VMEM((2 * MAIN, WIDTH), BF16),
            pltpu.SemaphoreType.DMA((SEMS,)),
            pltpu.SemaphoreType.DMA((SEMS,)),
            pltpu.SemaphoreType.DMA((6,)),
        ],
        compiler_params=pltpu.CompilerParams(
            collective_id=0, has_side_effects=True, vmem_limit_bytes=44 << 20
        ),
        name="head_step",
    )(teacher_feats.reshape(32, FEAT), student_feats.reshape(2 * MAIN, WIDTH), norm_gain, head_weight.reshape(128, WIDTH), slot_image.transpose(0, 1, 3, 2), slot_count)
    return (
        loss,
        sgrad.reshape(student_feats.shape),
        hgrad.reshape(1, 128, WIDTH),
        gain_grad,
    )


def solution(mesh):
    return jax.shard_map(
        shards,
        mesh=mesh,
        in_specs=(
            P("teacher", ("group", "dp"), None),
            P("group", "teacher", "dp", None, None, None),
            P("group", None),
            P("group", ("teacher", "dp"), None),
            P(None, "teacher", None, None),
            P(None, "teacher", None),
        ),
        out_specs=(
            P("group"),
            P("group", "teacher", "dp", None, None, None),
            P("group", ("teacher", "dp"), None),
            P("group", None),
        ),
        check_vma=False,
    )
```

```python
import jax
import jax.numpy as jnp
from jax import lax
from jax.experimental import pallas as pl
from jax.experimental.pallas import tpu as pltpu
from jax.sharding import PartitionSpec as P

MESH = pl.DeviceIdType.MESH
F32 = jnp.float32
BF16 = jnp.bfloat16

FEAT = 4096
WIDTH = 768
PATCHES = 256
SLICE = 1024
MAIN = 256
PART = 32
GROUP = 640
TOTAL = 32 * PATCHES
SEMS = 46


def permutation(size, source_of):
    rows = lax.broadcasted_iota(jnp.int32, (size, size), 0)
    cols = lax.broadcasted_iota(jnp.int32, (size, size), 1)
    return jnp.where(source_of(rows) == cols, 1.0, 0.0).astype(BF16)


def image_order(n):
    return (n // 4 % 4) * 32 + (n // 16) * 4 + n % 4


def dot(a, b, dims):
    return lax.dot_general(a, b, (dims, ((), ())), preferred_element_type=F32)


def kernel(
    teach, feats, gain, head, images, used_slots,
    loss_o, gain_o, sgrad_o, hgrad_o,
    arrived, near_target, far_target, heads, rows_b, extra_out, extra_in,
    xhat, rstd, logits, dlogits, sums, cols,
    stat_out, stat_in, tiny_out, tiny_in,
    g_out, g_own, g_in, gz_out, gz_in,
    d_all, d_out, d_in, relay_out, relay_in, e_in, e_all,
    feats_v, send_sem, recv_sem, local_sem,
):
    t = lax.axis_index("teacher")
    g = lax.axis_index("group")
    d = lax.axis_index("dp")
    x, zh = d // 2, d % 2
    zl, core = g // 2, g % 2
    z = zh * 4 + zl

    def device(dx=0, dy=0, dz=0, dc=0):
        to_z = (z + dz + 8) % 8
        return {
            "teacher": (t + dy + 4) % 4,
            "group": (to_z % 4) * 2 + (core + dc) % 2,
            "dp": ((x + dx + 4) % 4) * 2 + to_z // 4,
        }

    used = [0]

    def group(view):
        index = used[0]
        used[0] += 1
        return (index, view)

    def send(src, dst, to, into, sent=None):
        copy = pltpu.make_async_remote_copy(
            src_ref=src, dst_ref=dst, send_sem=send_sem.at[into[0] if sent is None else sent],
            recv_sem=recv_sem.at[into[0]], device_id=to, device_id_type=MESH,
        )
        copy.start()
        if sent is None and into[0] not in sent_views:
            sent_views[into[0]] = into[1]
        return copy

    sent_views = {}

    def arrive(into):
        pltpu.make_async_copy(into[1], into[1], recv_sem.at[into[0]]).wait()

    barrier = pltpu.get_barrier_semaphore()
    partners = [device(dx=k) for k in (1, 2, 3)] + [device(dy=k) for k in (1, 2, 3)]
    partners += [device(dz=k) for k in (1, -1, 4)] + [device(dc=1)]
    for to in partners:
        pl.semaphore_signal(barrier, inc=1, device_id=to, device_id_type=MESH)

    def patch_order(n):
        h, q, c, xs, p = n // 128, n // 32 % 4, n // 16 % 2, n // 4 % 4, n % 4
        away = jnp.where(q == 1, 7, jnp.where(q == 2, 1, jnp.where(q == 3, 6, 0)))
        at = (z + away + 4 * h) % 8
        return (at % 4) * 64 + c * 32 + xs * 8 + (at // 4) * 4 + p

    mine = t * 2 + zh
    feats_in = pltpu.make_async_copy(feats, feats_v, local_sem.at[0])
    feats_in.start()

    def columns_of(to, b):
        return pl.ds(pl.multiple_of(b * SLICE + to * 256, 256), 256)

    owned = [pltpu.make_async_copy(head, heads.at[mine], local_sem.at[1])]
    for b in range(4):
        owned.append(pltpu.make_async_copy(
            teach.at[:, columns_of(x, b)], arrived.at[x, :, pl.ds(b * 256, 256)], local_sem.at[2 + b]
        ))
    for copy in owned:
        copy.start()
    feats_in.wait()
    second = jnp.where(used_slots[g, 0, d] >= 2, 1.0, 0.0).astype(F32)
    order = permutation(MAIN, patch_order)
    for slot in range(2):
        part = pl.ds(slot * MAIN, MAIN)
        values = dot(order, feats_v[part, :], ((1,), (0,)))
        center = values - jnp.mean(values, axis=-1, keepdims=True)
        rs = lax.rsqrt(jnp.mean(center * center, axis=-1, keepdims=True) + 1e-06)
        unit = center * rs
        xhat[part, :] = unit
        rstd[part, :] = jnp.broadcast_to(rs, (MAIN, 128))
        normed = unit * gain[...]
        if slot == 0:
            rows_b[:, :, x] = normed.astype(BF16).reshape(2, 4, PART, WIDTH)
        else:
            extra_out[...] = (normed * second).astype(BF16).reshape(2, 4, PART, WIDTH)
    pl.semaphore_wait(barrier, len(partners))

    slices = group(arrived.at[pl.ds(0, 3)])
    for k in (1, 3, 2):
        for b in range(4):
            columns = columns_of((x + k) % 4, b)
            send(teach.at[:, columns], arrived.at[x, :, pl.ds(b * 256, 256)], device(dx=k), slices)
    head_z = group(head)
    send(head, heads.at[mine], device(dz=4), head_z)
    parts = group(extra_in)
    for k in (1, 3, 2):
        send(extra_out.at[:, (x + k) % 4], extra_in.at[k - 1], device(dx=k), parts)

    def rows_out(h):
        here = rows_b.at[h, :, x]
        into = group(rows_b.at[h, :, pl.ds(0, 2)])
        for k in (1, -1):
            send(here, here, device(dx=k), into)
        return into

    def rows_on(h, found):
        arrive(found)
        left, right = rows_b.at[h, pl.ds(0, 2), (x + 3) % 4], rows_b.at[h, pl.ds(2, 2), (x + 1) % 4]
        into = group(rows_b.at[h, :, 0])
        send(left, left, device(dx=1), into)
        send(right, right, device(dx=-1), into)
        return into

    def tails_out(h):
        tail = rows_b.at[h, x, 4]
        into = group(rows_b.at[h, pl.ds(0, 3), 4])
        for k in (1, 3, 2):
            send(tail, tail, device(dx=k), into)
        return into

    rows_a = rows_out(0)
    head_y = group(heads.at[pl.ds(0, 6)])
    for k in (1, 3, 2):
        send(head, heads.at[mine], device(dy=k), head_y)

    arrive(slices)
    for copy in owned:
        copy.wait()
    own = dot(permutation(128, image_order), arrived[...].reshape(128, SLICE), ((1,), (0,)))
    target = (near_target, far_target)
    near_target[0, :, core] = own.astype(BF16).reshape(8, 16, SLICE)
    places = {0: (0, 0), -1: (0, 1), 1: (0, 2), -2: (0, 3), 4: (1, 0), -4: (1, 0), 3: (1, 1), -3: (1, 2), 2: (1, 3)}

    def chunk(step, half):
        h, q = places[step]
        return target[h].at[q, pl.ds(half * 4, 4), core]

    shared = [group(target[h].at[:, :, 0]) for h in range(2)]
    chunks_sent = used[0]
    used[0] += 1
    sent_views[chunks_sent] = near_target.at[:, pl.ds(0, 7)]

    def pass_on(step, half, ways):
        piece = chunk(step, half)
        found = [send(piece, chunk(step - way, half), device(dz=way), group(piece), chunks_sent) for way in ways]
        send(piece, piece, device(dc=1), shared[places[step][0]])
        return found[0] if found else None

    def first_step():
        up, down = [None, None], [None, None]
        for half in range(2):
            up[half] = send(chunk(0, half), chunk(-1, half), device(dz=1), group(chunk(0, half)), chunks_sent)
            other = 1 - half
            down[other] = send(chunk(0, other), chunk(1, other), device(dz=-1), group(chunk(0, other)), chunks_sent)
        for half in range(2):
            pass_on(0, half, ())
        return up, down

    from_low, from_high = first_step()

    def ring_step(step, halves=(0, 1)):
        last = step == 3
        for half in halves:
            from_low[half].wait_recv()
            from_low[half] = pass_on(-step, half, () if last and half == 1 else (1,))
            other = 1 - half
            from_high[other].wait_recv()
            from_high[other] = pass_on(step, other, () if last and other == 0 else (-1,))

    arrive(parts)
    quarter = extra_out[:, x].astype(F32)
    quarter += extra_in[0].astype(F32) + extra_in[1].astype(F32) + extra_in[2].astype(F32)
    rows_b[:, x, 4] = quarter.astype(BF16)
    tails_a = tails_out(0)
    rows_b1 = rows_out(1)

    arrive(head_z)
    theirs = heads.at[t * 2 + 1 - zh]
    for k in (1, 3, 2):
        send(theirs, theirs, device(dy=k), head_y)

    ring_step(1, (0,))
    rows_a = rows_on(0, rows_a)
    tails_b = tails_out(1)
    ring_step(1, (1,))
    ring_step(2, (0,))
    rows_b1 = rows_on(1, rows_b1)
    ring_step(2, (1,))
    arrive(head_y)
    arrive(rows_a)
    arrive(tails_a)

    extra_image = jnp.int32(0)
    extra_weight = jnp.float32(0)
    image, weights = [], []
    for b in range(4):
        count = used_slots[g, 0, b * 2 + zh]
        twice = count >= 2
        extra_image += jnp.where(twice, images[g, 0, 1, b * 2 + zh], 0)
        extra_weight += jnp.where(twice, 1.0, 0.0).astype(F32)
        image.append(images[g, 0, 0, b * 2 + zh])
        weights.append(jnp.where(count >= 1, 1.0, 0.0).astype(F32))
    image.append(extra_image)
    weights.append(extra_weight)
    row = lax.broadcasted_iota(jnp.int32, (1, GROUP), 1)
    slot_of = (row // PART) % 5
    weight = jnp.zeros((1, GROUP), F32)
    for i in range(5):
        weight = jnp.where(slot_of == i, weights[i], weight)
    here = (slot_of == x) | ((slot_of == 4) & (row // 160 == x))
    loss = jnp.float32(0)

    def targets(h, q):
        found = [target[h][q, image[i]].reshape(PART, SLICE) for i in range(5)]
        return jnp.concatenate(found, axis=0).astype(F32)

    def forward(h):
        def step(b, carry):
            rows = rows_b[h, pl.ds(b * 2, 2)].reshape(320, WIDTH)
            out = dot(rows, heads[...].reshape(SLICE, WIDTH), ((1,), (1,)))
            logits[h, pl.ds(b * 2, 2)] = out.reshape(2, 160, SLICE)
            return carry

        lax.fori_loop(0, 2, step, 0)

    lane = lax.broadcasted_iota(jnp.int32, (160, 128), 1)

    def statistics(h):
        def step(q, carry):
            lg = logits[h, q]
            tg = targets(h, q)
            inner = jnp.sum(lg * tg, axis=-1, keepdims=True)
            lsq = jnp.sum(lg * lg, axis=-1, keepdims=True)
            tsq = jnp.sum(tg * tg, axis=-1, keepdims=True)
            at = pl.ds(pl.multiple_of(q * 160, 32), 160)
            sums[h, at, :] = jnp.where(lane == 0, inner, jnp.where(lane == 1, lsq, tsq))
            return carry

        lax.fori_loop(0, 4, step, 0)
        for k in range(GROUP // 128):
            at = pl.ds(k * 128, 128)
            stat_out[h, :, at] = jnp.transpose(sums[h, at, :])[:4]
        into = group(stat_in.at[:, h])
        for k in (1, 3, 2):
            send(stat_out.at[h], stat_in.at[k - 1, h], device(dx=k), into)
        return into

    def factors(h):
        total = (stat_out[h] + stat_in[0, h] + stat_in[1, h] + stat_in[2, h]) * (1.0 / FEAT)
        inner, lsq, tsq = total[0:1], total[1:2], total[2:3]
        rl, rt = lax.rsqrt(lsq + 1e-06), lax.rsqrt(tsq + 1e-06)
        on_target = weight * rl * rt * (-1.0 / 16.0)
        on_logits = weight * inner * rt * rl * rl * rl * (1.0 / 16.0)
        pair = jnp.concatenate([on_target, on_logits, jnp.zeros((126, GROUP), F32)], axis=0)
        for k in range(GROUP // 128):
            cols[h, k * 128:(k + 1) * 128, :] = jnp.transpose(pair[:, k * 128:(k + 1) * 128])

        def step(q, carry):
            found = cols[h, pl.ds(pl.multiple_of(q * 160, 32), 160), :]
            dl = found[:, 0:1] * targets(h, q) + found[:, 1:2] * logits[h, q]
            dlogits[h, q] = dl.astype(BF16)
            return carry

        lax.fori_loop(0, 4, step, 0)
        return jnp.sum(jnp.where(here, weight * (1.0 - inner * rl * rt), 0.0)) * (1.0 / TOTAL)

    def row_gradient(h):
        def step(b, carry):
            part = dot(dlogits[h, pl.ds(b * 2, 2)].reshape(320, SLICE), heads[...].reshape(SLICE, WIDTH), ((1,), (0,)))
            part = part.reshape(2, 5, PART, WIDTH)
            d_all[h, pl.ds(b * 2, 2)] = part
            d_out[h, pl.ds(b * 2, 2)] = part.astype(BF16)
            return carry

        lax.fori_loop(0, 2, step, 0)

    def send_rows(h):
        low, high = pl.ds(0, 2), pl.ds(2, 2)
        across = (x + 2) % 4
        relay = group(relay_in.at[:, h])
        send(d_out.at[h, low, across], relay_in.at[0, h], device(dx=1), relay)
        send(d_out.at[h, high, across], relay_in.at[1, h], device(dx=-1), relay)
        ext = group(e_in.at[:, h])
        for k in (1, 3, 2):
            send(d_out.at[h, (x + k) % 4, 4], e_in.at[k - 1, h], device(dx=k), ext)
        return relay, ext

    def send_plain(h):
        low, high = pl.ds(0, 2), pl.ds(2, 2)
        main = group(d_in.at[:, h])
        send(d_out.at[h, high, (x + 1) % 4], d_in.at[0, h, high], device(dx=1), main)
        send(d_out.at[h, low, (x + 3) % 4], d_in.at[1, h, low], device(dx=-1), main)
        return main

    def relay_on(h, relay, main):
        low, high = pl.ds(0, 2), pl.ds(2, 2)
        after, before = (x + 1) % 4, (x + 3) % 4
        arrive(relay)
        relay_out[0, h] = (d_all[h, low, after] + relay_in[0, h].astype(F32)).astype(BF16)
        send(relay_out.at[0, h], d_in.at[0, h, low], device(dx=1), main)
        relay_out[1, h] = (d_all[h, high, before] + relay_in[1, h].astype(F32)).astype(BF16)
        send(relay_out.at[1, h], d_in.at[1, h, high], device(dx=-1), main)

    def extra_sum(h, ext):
        arrive(ext)
        total = d_all[h, x, 4]
        for k in range(3):
            total += e_in[k, h].astype(F32)
        e_all[h, x] = total.astype(BF16)
        piece = e_all.at[h, x]
        into = group(e_all.at[h, pl.ds(0, 3)])
        for k in (1, 3, 2):
            send(piece, piece, device(dx=k), into)
        return into

    forward(0)
    arrive(shared[0])
    stats_a = statistics(0)
    ring_step(3, (0,))
    arrive(rows_b1)
    arrive(tails_b)
    forward(1)
    ring_step(3, (1,))
    arrive(stats_a)
    loss += factors(0)
    row_gradient(0)
    relay_a, ext_a = send_rows(0)
    from_low[0].wait_recv()
    pass_on(-4, 0, ())
    from_high[1].wait_recv()
    pass_on(4, 1, ())
    arrive(shared[1])
    stats_b = statistics(1)
    main_a = send_plain(0)
    arrive(stats_b)
    loss += factors(1)

    far, close = (1 - zh) * 128, zh * 128
    gain_part = jnp.zeros((1, WIDTH), F32)
    away = [group(g_in.at[:, pl.ds(0, 64)]) for _ in range(2)]
    near = group(g_in.at[:, pl.ds(0, 128)])

    def send_half(k, start, size, into):
        at = pl.ds(pl.multiple_of(start, 64), size)
        send(g_out.at[k - 1, at], g_in.at[k - 1, at], device(dy=k), into)

    for k in (1, 3, 2, 0):
        to = (t + k) % 4
        columns = pl.ds(pl.multiple_of(to * 256, 256), 256)
        part = dot(
            dlogits[:, :, :, columns].reshape(2 * GROUP, 256), rows_b[...].reshape(2 * GROUP, WIDTH), ((0,), (0,))
        )
        head_part = heads[pl.ds(to * 2, 2)].reshape(256, WIDTH).astype(F32)
        gain_part += jnp.sum(part * head_part, axis=0, keepdims=True)
        if k:
            g_out[k - 1] = part.astype(BF16)
            send_half(k, far, 64, away[0])
            send_half(k, far + 64, 64, away[1])
        else:
            g_own[...] = part
        if k == 3:
            relay_on(0, relay_a, main_a)
        if k == 2:
            for other in (1, 3, 2):
                send_half(other, close, 128, near)
            row_gradient(1)
            relay_b, ext_b = send_rows(1)
            main_b = send_plain(1)
            ext_all = [extra_sum(0, ext_a)]

    which = lax.broadcasted_iota(jnp.int32, (8, WIDTH), 0)
    tiny = jnp.where(which == 0, gain_part / gain[...], jnp.where(which == 1, loss, 0.0))
    tiny_out[0] = tiny
    tiny_z = group(tiny_in.at[6])
    send(tiny_out.at[0], tiny_in.at[6], device(dz=4), tiny_z)

    def rows_from_y(start, size):
        at = pl.ds(pl.multiple_of(start, 64), size)
        part = g_own[at, :]
        for k in range(3):
            part += g_in[k, at].astype(F32)
        return part

    relay_on(1, relay_b, main_b)
    arrive(tiny_z)
    tiny += tiny_in[6]
    tiny_out[1] = tiny
    tiny_x = group(tiny_in.at[pl.ds(0, 3)])
    for k in (1, 3, 2):
        send(tiny_out.at[1], tiny_in.at[k - 1], device(dx=k), tiny_x)
    across = []
    for c in range(2):
        arrive(away[c])
        at = pl.ds(c * 64, 64)
        gz_out[at, :] = rows_from_y(far + c * 64, 64).astype(BF16)
        across.append(group(gz_in.at[at]))
        send(gz_out.at[at], gz_in.at[at], device(dz=4), across[c])
        if c == 0:
            ext_all.append(extra_sum(1, ext_b))
    arrive(tiny_x)
    tiny += tiny_in[0] + tiny_in[1] + tiny_in[2]
    tiny_out[2] = tiny
    tiny_y = group(tiny_in.at[pl.ds(3, 3)])
    for k in (1, 3, 2):
        send(tiny_out.at[2], tiny_in.at[2 + k], device(dy=k), tiny_y)

    def finish(dnormed, part):
        dx = dnormed.reshape(MAIN, WIDTH) * gain[...]
        unit = xhat[part, :]
        drop = jnp.mean(dx, axis=-1, keepdims=True)
        along = jnp.mean(dx * unit, axis=-1, keepdims=True)
        out = (rstd[part, :][:, 0:1] * (dx - drop - unit * along)).astype(BF16)
        sgrad_o[part, :] = dot(order, out, ((0,), (0,))).astype(BF16)

    arrive(main_a)
    arrive(main_b)
    finish(d_all[:, :, x] + d_in[0].astype(F32) + d_in[1].astype(F32), pl.ds(0, MAIN))
    arrive(ext_all[0])
    arrive(ext_all[1])
    finish(e_all[...].astype(F32) * second, pl.ds(MAIN, MAIN))
    arrive(near)
    hgrad_o[...] = rows_from_y(close, 128)
    arrive(across[0])
    arrive(across[1])
    hgrad_o[...] += gz_in[...].astype(F32)
    arrive(tiny_y)
    tiny += tiny_in[3] + tiny_in[4] + tiny_in[5]
    gain_o[...] = tiny[0:1]
    loss_o[0] = tiny[1, 0]
    for index, view in sent_views.items():
        pltpu.make_async_copy(view, view, send_sem.at[index]).wait()


def shards(teacher_feats, student_feats, norm_gain, head_weight, slot_image, slot_count):
    vmem = pl.BlockSpec(memory_space=pltpu.VMEM)
    smem = pl.BlockSpec(memory_space=pltpu.SMEM)
    anywhere = pl.BlockSpec(memory_space=pl.ANY)
    loss, gain_grad, sgrad, hgrad = pl.pallas_call(
        kernel,
        out_shape=(
            jax.ShapeDtypeStruct((1,), F32),
            pltpu.VMEM((1, WIDTH), F32),
            pltpu.VMEM((2 * MAIN, WIDTH), BF16),
            pltpu.VMEM((128, WIDTH), F32),
        ),
        in_specs=[anywhere, anywhere, vmem, anywhere, smem, smem],
        out_specs=(smem, vmem, vmem, vmem),
        scratch_shapes=[
            pltpu.VMEM((4, 32, SLICE), BF16),
            pltpu.VMEM((4, 8, 2, 16, SLICE), BF16),
            pltpu.VMEM((4, 8, 2, 16, SLICE), BF16),
            pltpu.VMEM((8, 128, WIDTH), BF16),
            pltpu.VMEM((2, 4, 5, PART, WIDTH), BF16),
            pltpu.VMEM((2, 4, PART, WIDTH), BF16),
            pltpu.VMEM((3, 2, PART, WIDTH), BF16),
            pltpu.VMEM((2 * MAIN, WIDTH), F32),
            pltpu.VMEM((2 * MAIN, 128), F32),
            pltpu.VMEM((2, 4, 160, SLICE), F32),
            pltpu.VMEM((2, 4, 160, SLICE), BF16),
            pltpu.VMEM((2, GROUP, 128), F32),
            pltpu.VMEM((2, GROUP, 128), F32),
            pltpu.VMEM((2, 4, GROUP), F32),
            pltpu.VMEM((3, 2, 4, GROUP), F32),
            pltpu.VMEM((3, 8, WIDTH), F32),
            pltpu.VMEM((7, 8, WIDTH), F32),
            pltpu.VMEM((3, 256, WIDTH), BF16),
            pltpu.VMEM((256, WIDTH), F32),
            pltpu.VMEM((3, 256, WIDTH), BF16),
            pltpu.VMEM((128, WIDTH), BF16),
            pltpu.VMEM((128, WIDTH), BF16),
            pltpu.VMEM((2, 4, 5, PART, WIDTH), F32),
            pltpu.VMEM((2, 4, 5, PART, WIDTH), BF16),
            pltpu.VMEM((2, 2, 4, PART, WIDTH), BF16),
            pltpu.VMEM((2, 2, 2, PART, WIDTH), BF16),
            pltpu.VMEM((2, 2, 2, PART, WIDTH), BF16),
            pltpu.VMEM((3, 2, PART, WIDTH), BF16),
            pltpu.VMEM((2, 4, PART, WIDTH), BF16),
            pltpu.VMEM((2 * MAIN, WIDTH), BF16),
            pltpu.SemaphoreType.DMA((SEMS,)),
            pltpu.SemaphoreType.DMA((SEMS,)),
            pltpu.SemaphoreType.DMA((6,)),
        ],
        compiler_params=pltpu.CompilerParams(
            collective_id=0, has_side_effects=True, vmem_limit_bytes=44 << 20
        ),
        name="head_step",
    )(teacher_feats.reshape(32, FEAT), student_feats.reshape(2 * MAIN, WIDTH), norm_gain, head_weight.reshape(128, WIDTH), slot_image.transpose(0, 1, 3, 2), slot_count)
    return (
        loss,
        sgrad.reshape(student_feats.shape),
        hgrad.reshape(1, 128, WIDTH),
        gain_grad,
    )


def solution(mesh):
    return jax.shard_map(
        shards,
        mesh=mesh,
        in_specs=(
            P("teacher", ("group", "dp"), None),
            P("group", "teacher", "dp", None, None, None),
            P("group", None),
            P("group", ("teacher", "dp"), None),
            P(None, "teacher", None, None),
            P(None, "teacher", None),
        ),
        out_specs=(
            P("group"),
            P("group", "teacher", "dp", None, None, None),
            P("group", ("teacher", "dp"), None),
            P("group", None),
        ),
        check_vma=False,
    )
```

```python
import jax
import jax.numpy as jnp
from jax import lax
from jax.experimental import pallas as pl
from jax.experimental.pallas import tpu as pltpu
from jax.sharding import PartitionSpec as P

MESH = pl.DeviceIdType.MESH
F32 = jnp.float32
BF16 = jnp.bfloat16

FEAT = 4096
WIDTH = 768
PATCHES = 256
SLICE = 1024
MAIN = 256
PART = 32
GROUP = 640
TOTAL = 32 * PATCHES
RECV_SEMS, SEND_SEMS = 45, 32


def permutation(size, source_of):
    rows = lax.broadcasted_iota(jnp.int32, (size, size), 0)
    cols = lax.broadcasted_iota(jnp.int32, (size, size), 1)
    return jnp.where(source_of(rows) == cols, 1.0, 0.0).astype(BF16)


def image_order(n):
    return (n // 4 % 4) * 32 + (n // 16) * 4 + n % 4


def dot(a, b, dims):
    return lax.dot_general(a, b, (dims, ((), ())), preferred_element_type=F32)


def kernel(
    teach, feats, gain_h, head, images_h, used_slots_h,
    loss_o, gain_o, sgrad_o, hgrad_o,
    arrived, near_target, far_target, heads, rows_b, extra_out, extra_in,
    xhat, rstd, logits, dlogits, sums, cols,
    stat_out, stat_in, tiny_out, tiny_in, g_near,
    g_out, g_own, g_in, y_relay, y_sum, n_in, gz_out, gz_in,
    d_all, d_out, d_in, relay_out, relay_in, e_in, e_all,
    feats_v, gain, images, used_slots, send_sem, recv_sem, local_sem,
):
    t = lax.axis_index("teacher")
    g = lax.axis_index("group")
    d = lax.axis_index("dp")
    x, zh = d // 2, d % 2
    zl, core = g // 2, g % 2
    z = zh * 4 + zl

    def device(dx=0, dy=0, dz=0, dc=0):
        to_z = (z + dz + 8) % 8
        return {
            "teacher": (t + dy + 4) % 4,
            "group": (to_z % 4) * 2 + (core + dc) % 2,
            "dp": ((x + dx + 4) % 4) * 2 + to_z // 4,
        }

    used = [0, 0]

    def group(view):
        index = used[0]
        used[0] += 1
        return (index, view)

    def send(src, dst, to, into, sent=None):
        if sent is None:
            if into[0] not in sent_by:
                sent_by[into[0]] = used[1]
                sent_views[used[1]] = into[1]
                used[1] += 1
            sent = sent_by[into[0]]
        copy = pltpu.make_async_remote_copy(
            src_ref=src, dst_ref=dst, send_sem=send_sem.at[sent],
            recv_sem=recv_sem.at[into[0]], device_id=to, device_id_type=MESH,
        )
        copy.start()
        return copy

    sent_by, sent_views = {}, {}

    def arrive(into):
        pltpu.make_async_copy(into[1], into[1], recv_sem.at[into[0]]).wait()

    barrier = pltpu.get_barrier_semaphore()
    partners = [device(dx=k) for k in (1, 2, 3)] + [device(dy=k) for k in (1, 2, 3)]
    partners += [device(dz=k) for k in (1, -1, 4)] + [device(dc=1)]
    for to in partners:
        pl.semaphore_signal(barrier, inc=1, device_id=to, device_id_type=MESH)

    def patch_order(n):
        h, q, c, xs, p = n // 128, n // 32 % 4, n // 16 % 2, n // 4 % 4, n % 4
        away = jnp.where(q == 1, 7, jnp.where(q == 2, 1, jnp.where(q == 3, 6, 0)))
        at = (z + away + 4 * h) % 8
        return (at % 4) * 64 + c * 32 + xs * 8 + (at // 4) * 4 + p

    mine = t * 2 + zh
    inputs = [
        pltpu.make_async_copy(src, dst, local_sem.at[6 + n])
        for n, (src, dst) in enumerate(((images_h, images), (used_slots_h, used_slots), (gain_h, gain), (feats, feats_v)))
    ]
    for copy in inputs:
        copy.start()

    def columns_of(to, b):
        return pl.ds(pl.multiple_of(b * SLICE + to * 256, 256), 256)

    owned = [pltpu.make_async_copy(head, heads.at[mine], local_sem.at[1])]
    for b in range(4):
        owned.append(pltpu.make_async_copy(
            teach.at[:, :, columns_of(x, b)], arrived.at[x, :, :, pl.ds(b * 256, 256)], local_sem.at[2 + b]
        ))
    for copy in owned:
        copy.start()
    for copy in inputs:
        copy.wait()
    second = jnp.where(used_slots[g, 0, d] >= 2, 1.0, 0.0).astype(F32)
    order = permutation(MAIN, patch_order)
    for slot in range(2):
        part = pl.ds(slot * MAIN, MAIN)
        values = dot(order, feats_v[part, :], ((1,), (0,)))
        center = values - jnp.mean(values, axis=-1, keepdims=True)
        rs = lax.rsqrt(jnp.mean(center * center, axis=-1, keepdims=True) + 1e-06)
        unit = center * rs
        xhat[part, :] = unit
        rstd[part, :] = jnp.broadcast_to(rs, (MAIN, 128))
        normed = unit * gain[...]
        if slot == 0:
            rows_b[:, :, x] = normed.astype(BF16).reshape(2, 4, PART, WIDTH)
        else:
            extra_out[...] = (normed * second).astype(BF16).reshape(2, 4, PART, WIDTH)
    pl.semaphore_wait(barrier, len(partners))

    slices = group(arrived.at[pl.ds(0, 3)])
    for k in (1, 3, 2):
        for b in range(4):
            columns = columns_of((x + k) % 4, b)
            send(teach.at[:, :, columns], arrived.at[x, :, :, pl.ds(b * 256, 256)], device(dx=k), slices)
    head_z = group(head)
    send(head, heads.at[mine], device(dz=4), head_z)
    head_y = group(heads.at[pl.ds(0, 6)])
    for k in (1, 3, 2):
        send(head, heads.at[mine], device(dy=k), head_y)
    parts = group(extra_in)
    for k in (1, 3, 2):
        send(extra_out.at[:, (x + k) % 4], extra_in.at[k - 1], device(dx=k), parts)

    def rows_out(h):
        here = rows_b.at[h, :, x]
        into = group(rows_b.at[h, :, pl.ds(0, 2)])
        for k in (1, -1):
            send(here, here, device(dx=k), into)
        return into

    def rows_on(h, found):
        arrive(found)
        left, right = rows_b.at[h, pl.ds(0, 2), (x + 3) % 4], rows_b.at[h, pl.ds(2, 2), (x + 1) % 4]
        into = group(rows_b.at[h, :, 0])
        send(left, left, device(dx=1), into)
        send(right, right, device(dx=-1), into)
        return into

    def tails_out(h):
        tail = rows_b.at[h, x, 4]
        into = group(rows_b.at[h, pl.ds(0, 3), 4])
        for k in (1, 3, 2):
            send(tail, tail, device(dx=k), into)
        return into

    rows_a = rows_out(0)

    arrive(slices)
    for copy in owned:
        copy.wait()
    own = dot(permutation(128, image_order), arrived[...].astype(F32).reshape(128, SLICE).astype(BF16), ((1,), (0,)))
    target = (near_target, far_target)
    near_target[0, :, core] = own.astype(BF16).reshape(8, 16, SLICE)
    places = {0: (0, 0), -1: (0, 1), 1: (0, 2), -2: (0, 3), 4: (1, 0), -4: (1, 0), 3: (1, 1), -3: (1, 2), 2: (1, 3)}

    def chunk(step, half):
        h, q = places[step]
        return target[h].at[q, pl.ds(half * 4, 4), core]

    shared = [group(target[h].at[:, :, 0]) for h in range(2)]
    chunks_sent = used[1]
    used[1] += 1
    sent_views[chunks_sent] = near_target.at[:, pl.ds(0, 7)]

    def pass_on(step, half, ways):
        piece = chunk(step, half)
        found = [send(piece, chunk(step - way, half), device(dz=way), group(piece), chunks_sent) for way in ways]
        send(piece, piece, device(dc=1), shared[places[step][0]])
        return found[0] if found else None

    def first_step():
        up, down = [None, None], [None, None]
        for half in range(2):
            up[half] = send(chunk(0, half), chunk(-1, half), device(dz=1), group(chunk(0, half)), chunks_sent)
            other = 1 - half
            down[other] = send(chunk(0, other), chunk(1, other), device(dz=-1), group(chunk(0, other)), chunks_sent)
        for half in range(2):
            pass_on(0, half, ())
        return up, down

    from_low, from_high = first_step()

    def ring_step(step, halves=(0, 1)):
        last = step == 3
        for half in halves:
            from_low[half].wait_recv()
            from_low[half] = pass_on(-step, half, () if last and half == 1 else (1,))
            other = 1 - half
            from_high[other].wait_recv()
            from_high[other] = pass_on(step, other, () if last and other == 0 else (-1,))

    arrive(parts)
    quarter = extra_out[:, x].astype(F32)
    quarter += extra_in[0].astype(F32) + extra_in[1].astype(F32) + extra_in[2].astype(F32)
    rows_b[:, x, 4] = quarter.astype(BF16)
    tails_a = tails_out(0)
    rows_b1 = rows_out(1)

    arrive(head_z)
    theirs = heads.at[t * 2 + 1 - zh]
    for k in (1, 3, 2):
        send(theirs, theirs, device(dy=k), head_y)

    ring_step(1, (0,))
    rows_a = rows_on(0, rows_a)
    tails_b = tails_out(1)
    ring_step(1, (1,))
    ring_step(2, (0,))
    rows_b1 = rows_on(1, rows_b1)
    ring_step(2, (1,))
    arrive(head_y)
    arrive(rows_a)
    arrive(tails_a)

    extra_image = jnp.int32(0)
    extra_weight = jnp.float32(0)
    image, weights = [], []
    for b in range(4):
        count = used_slots[g, 0, b * 2 + zh]
        twice = count >= 2
        extra_image += jnp.where(twice, images[g, 0, 1, b * 2 + zh], 0)
        extra_weight += jnp.where(twice, 1.0, 0.0).astype(F32)
        image.append(images[g, 0, 0, b * 2 + zh])
        weights.append(jnp.where(count >= 1, 1.0, 0.0).astype(F32))
    image.append(extra_image)
    weights.append(extra_weight)
    row = lax.broadcasted_iota(jnp.int32, (1, GROUP), 1)
    slot_of = (row // PART) % 5
    weight = jnp.zeros((1, GROUP), F32)
    for i in range(5):
        weight = jnp.where(slot_of == i, weights[i], weight)
    here = (slot_of == x) | ((slot_of == 4) & (row // 160 == x))
    loss = jnp.float32(0)

    def targets(h, q):
        found = [target[h][q, image[i]].reshape(PART, SLICE) for i in range(5)]
        return jnp.concatenate(found, axis=0).astype(F32)

    def forward(h):
        def step(b, carry):
            rows = rows_b[h, pl.ds(b * 2, 2)].reshape(320, WIDTH)
            out = dot(rows, heads[...].reshape(SLICE, WIDTH), ((1,), (1,)))
            logits[h, pl.ds(b * 2, 2)] = out.reshape(2, 160, SLICE)
            return carry

        lax.fori_loop(0, 2, step, 0)

    lane = lax.broadcasted_iota(jnp.int32, (160, 128), 1)

    def statistics(h):
        def step(q, carry):
            lg = logits[h, q]
            tg = targets(h, q)
            inner = jnp.sum(lg * tg, axis=-1, keepdims=True)
            lsq = jnp.sum(lg * lg, axis=-1, keepdims=True)
            tsq = jnp.sum(tg * tg, axis=-1, keepdims=True)
            at = pl.ds(pl.multiple_of(q * 160, 32), 160)
            sums[h, at, :] = jnp.where(lane == 0, inner, jnp.where(lane == 1, lsq, tsq))
            return carry

        lax.fori_loop(0, 4, step, 0)
        for k in range(GROUP // 128):
            at = pl.ds(k * 128, 128)
            stat_out[h, :, at] = jnp.transpose(sums[h, at, :])[:4]
        into = group(stat_in.at[:, h])
        for k in (1, 3, 2):
            send(stat_out.at[h], stat_in.at[k - 1, h], device(dx=k), into)
        return into

    def factors(h):
        total = (stat_out[h] + stat_in[0, h] + stat_in[1, h] + stat_in[2, h]) * (1.0 / FEAT)
        inner, lsq, tsq = total[0:1], total[1:2], total[2:3]
        rl, rt = lax.rsqrt(lsq + 1e-06), lax.rsqrt(tsq + 1e-06)
        on_target = weight * rl * rt * (-1.0 / 16.0)
        on_logits = weight * inner * rt * rl * rl * rl * (1.0 / 16.0)
        pair = jnp.concatenate([on_target, on_logits, jnp.zeros((126, GROUP), F32)], axis=0)
        for k in range(GROUP // 128):
            cols[h, k * 128:(k + 1) * 128, :] = jnp.transpose(pair[:, k * 128:(k + 1) * 128])

        def step(q, carry):
            found = cols[h, pl.ds(pl.multiple_of(q * 160, 32), 160), :]
            dl = found[:, 0:1] * targets(h, q) + found[:, 1:2] * logits[h, q]
            dlogits[h, q] = dl.astype(BF16)
            return carry

        lax.fori_loop(0, 4, step, 0)
        return jnp.sum(jnp.where(here, weight * (1.0 - inner * rl * rt), 0.0)) * (1.0 / TOTAL)

    def row_gradient(h):
        def step(b, carry):
            part = dot(dlogits[h, pl.ds(b * 2, 2)].reshape(320, SLICE), heads[...].reshape(SLICE, WIDTH), ((1,), (0,)))
            part = part.reshape(2, 5, PART, WIDTH)
            d_all[h, pl.ds(b * 2, 2)] = part
            d_out[h, pl.ds(b * 2, 2)] = part.astype(BF16)
            return carry

        lax.fori_loop(0, 2, step, 0)

    def send_rows(h):
        low, high = pl.ds(0, 2), pl.ds(2, 2)
        across = (x + 2) % 4
        relay = group(relay_in.at[:, h])
        send(d_out.at[h, low, across], relay_in.at[0, h], device(dx=1), relay)
        send(d_out.at[h, high, across], relay_in.at[1, h], device(dx=-1), relay)
        return relay

    def send_extra(h):
        ext = group(e_in.at[:, h])
        for k in (1, 3, 2):
            send(d_out.at[h, (x + k) % 4, 4], e_in.at[k - 1, h], device(dx=k), ext)
        return ext

    def send_plain(h):
        low, high = pl.ds(0, 2), pl.ds(2, 2)
        main = group(d_in.at[:, h])
        send(d_out.at[h, high, (x + 1) % 4], d_in.at[0, h, high], device(dx=1), main)
        send(d_out.at[h, low, (x + 3) % 4], d_in.at[1, h, low], device(dx=-1), main)
        return main

    def relay_on(h, relay, main):
        low, high = pl.ds(0, 2), pl.ds(2, 2)
        after, before = (x + 1) % 4, (x + 3) % 4
        arrive(relay)
        relay_out[0, h] = (d_all[h, low, after] + relay_in[0, h].astype(F32)).astype(BF16)
        send(relay_out.at[0, h], d_in.at[0, h, low], device(dx=1), main)
        relay_out[1, h] = (d_all[h, high, before] + relay_in[1, h].astype(F32)).astype(BF16)
        send(relay_out.at[1, h], d_in.at[1, h, high], device(dx=-1), main)

    def extra_sum(h, ext):
        arrive(ext)
        total = d_all[h, x, 4]
        for k in range(3):
            total += e_in[k, h].astype(F32)
        e_all[h, x] = total.astype(BF16)
        piece = e_all.at[h, x]
        into = group(e_all.at[h, pl.ds(0, 3)])
        for k in (1, 3, 2):
            send(piece, piece, device(dx=k), into)
        return into

    forward(0)
    arrive(shared[0])
    stats_a = statistics(0)
    ring_step(3, (0,))
    arrive(rows_b1)
    arrive(tails_b)
    forward(1)
    ring_step(3, (1,))
    arrive(stats_a)
    loss += factors(0)
    from_low[0].wait_recv()
    pass_on(-4, 0, ())
    from_high[1].wait_recv()
    pass_on(4, 1, ())
    row_gradient(0)
    relay_a = send_rows(0)
    arrive(shared[1])
    stats_b = statistics(1)

    def head_part(h, columns):
        lhs = dlogits[h, :, :, columns].reshape(GROUP, 256)
        return dot(lhs, rows_b[h].reshape(GROUP, WIDTH), ((0,), (0,)))

    def columns_for(k):
        return pl.ds(pl.multiple_of((t + k) % 4 * 256, 256), 256)

    for k in (1, 3, 2, 0):
        g_near[k] = head_part(0, columns_for(k))
    ext_a = send_extra(0)
    main_a = send_plain(0)
    arrive(stats_b)
    loss += factors(1)

    far, close = (1 - zh) * 128, zh * 128
    gain_part = jnp.zeros((1, WIDTH), F32)
    away = [group(g_in.at[:, pl.ds(0, 64)]) for _ in range(2)]
    near = group(n_in)
    turned = group(y_relay)

    def send_half(k, start, size, into):
        at = pl.ds(pl.multiple_of(start, 64), size)
        send(g_out.at[k - 1, at], g_in.at[k - 1, at], device(dy=k), into)

    for k in (1, 3, 2, 0):
        to = (t + k) % 4
        part = g_near[k] + head_part(1, columns_for(k))
        weights = heads[pl.ds(to * 2, 2)].reshape(256, WIDTH).astype(F32)
        gain_part += jnp.sum(part * weights, axis=0, keepdims=True)
        if k:
            g_out[k - 1] = part.astype(BF16)
            send_half(k, far, 64, away[0])
            send_half(k, far + 64, 64, away[1])
            g_near[k] = part
        else:
            g_own[...] = part
        if k == 3:
            relay_on(0, relay_a, main_a)

    which = lax.broadcasted_iota(jnp.int32, (2, WIDTH), 0)
    tiny = jnp.where(which == 0, gain_part / gain[...], loss)
    tiny_out[0] = tiny
    tiny_x = group(tiny_in.at[pl.ds(0, 3)])
    for k in (1, 3, 2):
        send(tiny_out.at[0], tiny_in.at[k - 1], device(dx=k), tiny_x)
    row_gradient(1)
    relay_b = send_rows(1)
    ext_b = send_extra(1)
    main_b = send_plain(1)
    ext_all = [extra_sum(0, ext_a)]
    arrive(tiny_x)
    tiny += tiny_in[0] + tiny_in[1] + tiny_in[2]
    tiny_out[1] = tiny
    tiny_y = group(tiny_in.at[pl.ds(3, 3)])
    for k in (1, 3, 2):
        send(tiny_out.at[1], tiny_in.at[2 + k], device(dy=k), tiny_y)
    def rows_from_y(start, size):
        at = pl.ds(pl.multiple_of(start, 64), size)
        part = g_own[at, :]
        for k in range(3):
            part += g_in[k, at].astype(F32)
        return part

    relay_on(1, relay_b, main_b)
    across = []
    for c in range(2):
        arrive(away[c])
        at = pl.ds(c * 64, 64)
        gz_out[at, :] = rows_from_y(far + c * 64, 64).astype(BF16)
        across.append(group(gz_in.at[at]))
        send(gz_out.at[at], gz_in.at[at], device(dz=4), across[c])
        if c == 0:
            at = pl.ds(pl.multiple_of(close, 64), 64)
            send(g_out.at[1, at], y_relay.at[0], device(dy=1), turned)
            at = pl.ds(pl.multiple_of(close + 64, 64), 64)
            send(g_out.at[1, at], y_relay.at[1], device(dy=-1), turned)
            send(g_out.at[0, at], n_in.at[0, pl.ds(64, 64)], device(dy=1), near)
            at = pl.ds(pl.multiple_of(close, 64), 64)
            send(g_out.at[2, at], n_in.at[1, pl.ds(0, 64)], device(dy=-1), near)
    ext_all.append(extra_sum(1, ext_b))
    arrive(turned)
    at = pl.ds(pl.multiple_of(close, 64), 64)
    y_sum[0] = (g_near[1, at, :] + y_relay[0].astype(F32)).astype(BF16)
    send(y_sum.at[0], n_in.at[0, pl.ds(0, 64)], device(dy=1), near)
    at = pl.ds(pl.multiple_of(close + 64, 64), 64)
    y_sum[1] = (g_near[3, at, :] + y_relay[1].astype(F32)).astype(BF16)
    send(y_sum.at[1], n_in.at[1, pl.ds(64, 64)], device(dy=-1), near)
    arrive(tiny_y)
    tiny += tiny_in[3] + tiny_in[4] + tiny_in[5]
    tiny_out[2] = tiny
    tiny_z = group(tiny_in.at[6])
    send(tiny_out.at[2], tiny_in.at[6], device(dz=4), tiny_z)

    def finish(dnormed, part):
        dx = dnormed.reshape(MAIN, WIDTH) * gain[...]
        unit = xhat[part, :]
        drop = jnp.mean(dx, axis=-1, keepdims=True)
        along = jnp.mean(dx * unit, axis=-1, keepdims=True)
        out = (rstd[part, :][:, 0:1] * (dx - drop - unit * along)).astype(BF16)
        sgrad_o[part, :] = dot(order, out, ((0,), (0,))).astype(BF16)

    arrive(main_a)
    arrive(main_b)
    finish(d_all[:, :, x] + d_in[0].astype(F32) + d_in[1].astype(F32), pl.ds(0, MAIN))
    arrive(ext_all[0])
    arrive(ext_all[1])
    finish(e_all[...].astype(F32) * second, pl.ds(MAIN, MAIN))
    arrive(near)
    hgrad_o[...] = g_own[pl.ds(pl.multiple_of(close, 64), 128), :] + n_in[0].astype(F32) + n_in[1].astype(F32)
    arrive(across[0])
    arrive(across[1])
    hgrad_o[...] += gz_in[...].astype(F32)
    arrive(tiny_z)
    tiny += tiny_in[6]
    gain_o[...] = tiny[0:1]
    loss_o[0] = tiny[1, 0]
    assert used == [RECV_SEMS, SEND_SEMS], used
    for index, view in sent_views.items():
        pltpu.make_async_copy(view, view, send_sem.at[index]).wait()


def shards(teacher_feats, student_feats, norm_gain, head_weight, slot_image, slot_count):
    vmem = pl.BlockSpec(memory_space=pltpu.VMEM)
    smem = pl.BlockSpec(memory_space=pltpu.SMEM)
    anywhere = pl.BlockSpec(memory_space=pl.ANY)
    operands = (
        teacher_feats, student_feats.reshape(2 * MAIN, WIDTH), norm_gain, head_weight.reshape(128, WIDTH),
        slot_image.transpose(0, 1, 3, 2), slot_count,
    )
    loss, gain_grad, sgrad, hgrad = pl.pallas_call(
        kernel,
        out_shape=(
            jax.ShapeDtypeStruct((1,), F32),
            pltpu.VMEM((1, WIDTH), F32),
            pltpu.VMEM((2 * MAIN, WIDTH), BF16),
            pltpu.VMEM((128, WIDTH), F32),
        ),
        in_specs=[anywhere] * 6,
        out_specs=(smem, vmem, vmem, vmem),
        scratch_shapes=[
            pltpu.VMEM((4, 8, 4, SLICE), BF16),
            pltpu.VMEM((4, 8, 2, 16, SLICE), BF16),
            pltpu.VMEM((4, 8, 2, 16, SLICE), BF16),
            pltpu.VMEM((8, 128, WIDTH), BF16),
            pltpu.VMEM((2, 4, 5, PART, WIDTH), BF16),
            pltpu.VMEM((2, 4, PART, WIDTH), BF16),
            pltpu.VMEM((3, 2, PART, WIDTH), BF16),
            pltpu.VMEM((2 * MAIN, WIDTH), F32),
            pltpu.VMEM((2 * MAIN, 128), F32),
            pltpu.VMEM((2, 4, 160, SLICE), F32),
            pltpu.VMEM((2, 4, 160, SLICE), BF16),
            pltpu.VMEM((2, GROUP, 128), F32),
            pltpu.VMEM((2, GROUP, 128), F32),
            pltpu.VMEM((2, 4, GROUP), F32),
            pltpu.VMEM((3, 2, 4, GROUP), F32),
            pltpu.VMEM((3, 2, WIDTH), F32),
            pltpu.VMEM((7, 2, WIDTH), F32),
            pltpu.VMEM((4, 256, WIDTH), F32),
            pltpu.VMEM((3, 256, WIDTH), BF16),
            pltpu.VMEM((256, WIDTH), F32),
            pltpu.VMEM((3, 256, WIDTH), BF16),
            pltpu.VMEM((2, 64, WIDTH), BF16),
            pltpu.VMEM((2, 64, WIDTH), BF16),
            pltpu.VMEM((2, 128, WIDTH), BF16),
            pltpu.VMEM((128, WIDTH), BF16),
            pltpu.VMEM((128, WIDTH), BF16),
            pltpu.VMEM((2, 4, 5, PART, WIDTH), F32),
            pltpu.VMEM((2, 4, 5, PART, WIDTH), BF16),
            pltpu.VMEM((2, 2, 4, PART, WIDTH), BF16),
            pltpu.VMEM((2, 2, 2, PART, WIDTH), BF16),
            pltpu.VMEM((2, 2, 2, PART, WIDTH), BF16),
            pltpu.VMEM((3, 2, PART, WIDTH), BF16),
            pltpu.VMEM((2, 4, PART, WIDTH), BF16),
            pltpu.VMEM((2 * MAIN, WIDTH), BF16),
            pltpu.VMEM((1, WIDTH), F32),
            pltpu.SMEM((8, 1, 2, 8), jnp.int32),
            pltpu.SMEM((8, 1, 8), jnp.int32),
            pltpu.SemaphoreType.DMA((SEND_SEMS,)),
            pltpu.SemaphoreType.DMA((RECV_SEMS,)),
            pltpu.SemaphoreType.DMA((10,)),
        ],
        compiler_params=pltpu.CompilerParams(
            collective_id=0, has_side_effects=True, vmem_limit_bytes=44 << 20
        ),
        name="head_step",
    )(*[pltpu.with_memory_space_constraint(operand, pltpu.HBM) for operand in operands])
    return (
        loss,
        sgrad.reshape(student_feats.shape),
        hgrad.reshape(1, 128, WIDTH),
        gain_grad,
    )


def solution(mesh):
    return jax.shard_map(
        shards,
        mesh=mesh,
        in_specs=(
            P("teacher", ("group", "dp"), None),
            P("group", "teacher", "dp", None, None, None),
            P("group", None),
            P("group", ("teacher", "dp"), None),
            P(None, "teacher", None, None),
            P(None, "teacher", None),
        ),
        out_specs=(
            P("group"),
            P("group", "teacher", "dp", None, None, None),
            P("group", ("teacher", "dp"), None),
            P("group", None),
        ),
        check_vma=False,
    )
```

```python
import jax
import jax.numpy as jnp
from jax import lax
from jax.experimental import pallas as pl
from jax.experimental.pallas import tpu as pltpu
from jax.sharding import PartitionSpec as P

MESH = pl.DeviceIdType.MESH
F32 = jnp.float32
BF16 = jnp.bfloat16

FEAT = 4096
WIDTH = 768
PATCHES = 256
SLICE = 1024
MAIN = 256
PART = 32
GROUP = 640
TOTAL = 32 * PATCHES
RECV_SEMS, SEND_SEMS = 45, 32


def permutation(size, source_of):
    rows = lax.broadcasted_iota(jnp.int32, (size, size), 0)
    cols = lax.broadcasted_iota(jnp.int32, (size, size), 1)
    return jnp.where(source_of(rows) == cols, 1.0, 0.0).astype(BF16)


def image_order(n):
    return (n // 4 % 4) * 32 + (n // 16) * 4 + n % 4


def dot(a, b, dims):
    return lax.dot_general(a, b, (dims, ((), ())), preferred_element_type=F32)


def kernel(
    teach, feats, gain_h, head, images_h, used_slots_h,
    loss_o, gain_o, sgrad_o, hgrad_o,
    arrived, near_target, far_target, heads, rows_b, extra_out, extra_in,
    xhat, rstd, logits, dlogits, sums, cols,
    stat_out, stat_in, tiny_out, tiny_in, g_near,
    g_out, g_own, g_in, y_relay, y_sum, n_in, gz_out, gz_in,
    d_all, d_out, d_in, relay_out, relay_in, e_in, e_all,
    feats_v, gain, images, used_slots, send_sem, recv_sem, local_sem,
):
    t = lax.axis_index("teacher")
    g = lax.axis_index("group")
    d = lax.axis_index("dp")
    x, zh = d // 2, d % 2
    zl, core = g // 2, g % 2
    z = zh * 4 + zl

    def device(dx=0, dy=0, dz=0, dc=0):
        to_z = (z + dz + 8) % 8
        return {
            "teacher": (t + dy + 4) % 4,
            "group": (to_z % 4) * 2 + (core + dc) % 2,
            "dp": ((x + dx + 4) % 4) * 2 + to_z // 4,
        }

    used = [0, 0]

    def group(view):
        index = used[0]
        used[0] += 1
        return (index, view)

    def send(src, dst, to, into, sent=None):
        if sent is None:
            if into[0] not in sent_by:
                sent_by[into[0]] = used[1]
                sent_views[used[1]] = into[1]
                used[1] += 1
            sent = sent_by[into[0]]
        copy = pltpu.make_async_remote_copy(
            src_ref=src, dst_ref=dst, send_sem=send_sem.at[sent],
            recv_sem=recv_sem.at[into[0]], device_id=to, device_id_type=MESH,
        )
        copy.start()
        return copy

    sent_by, sent_views = {}, {}

    def arrive(into):
        pltpu.make_async_copy(into[1], into[1], recv_sem.at[into[0]]).wait()

    barrier = pltpu.get_barrier_semaphore()
    partners = [device(dx=k) for k in (1, 2, 3)] + [device(dy=k) for k in (1, 2, 3)]
    partners += [device(dz=k) for k in (1, -1, 4)] + [device(dc=1)]
    for to in partners:
        pl.semaphore_signal(barrier, inc=1, device_id=to, device_id_type=MESH)

    def patch_order(n):
        h, q, c, xs, p = n // 128, n // 32 % 4, n // 16 % 2, n // 4 % 4, n % 4
        away = jnp.where(q == 1, 7, jnp.where(q == 2, 1, jnp.where(q == 3, 6, 0)))
        at = (z + away + 4 * h) % 8
        return (at % 4) * 64 + c * 32 + xs * 8 + (at // 4) * 4 + p

    mine = t * 2 + zh
    inputs = [
        pltpu.make_async_copy(src, dst, local_sem.at[3 + n])
        for n, (src, dst) in enumerate(((images_h, images), (used_slots_h, used_slots), (gain_h, gain), (feats, feats_v)))
    ]
    for copy in inputs:
        copy.start()

    def columns_of(to, b):
        return pl.ds(pl.multiple_of(b * SLICE + to * 256, 256), 256)

    owned = [pltpu.make_async_copy(head, heads.at[mine], local_sem.at[1])]
    own_columns = [
        pltpu.make_async_copy(
            teach.at[:, :, columns_of(x, b)], arrived.at[x, :, :, pl.ds(b * 256, 256)], local_sem.at[2]
        )
        for b in range(4)
    ]
    for copy in own_columns:
        copy.start()
    owned.append(pltpu.make_async_copy(arrived.at[x], arrived.at[x], local_sem.at[2]))
    owned[0].start()
    for copy in inputs:
        copy.wait()
    second = jnp.where(used_slots[g, 0, d] >= 2, 1.0, 0.0).astype(F32)
    order = permutation(MAIN, patch_order)
    for slot in range(2):
        part = pl.ds(slot * MAIN, MAIN)
        values = dot(order, feats_v[part, :], ((1,), (0,)))
        center = values - jnp.mean(values, axis=-1, keepdims=True)
        rs = lax.rsqrt(jnp.mean(center * center, axis=-1, keepdims=True) + 1e-06)
        unit = center * rs
        xhat[part, :] = unit
        rstd[part, :] = jnp.broadcast_to(rs, (MAIN, 128))
        normed = unit * gain[...]
        if slot == 0:
            rows_b[:, :, x] = normed.astype(BF16).reshape(2, 4, PART, WIDTH)
        else:
            extra_out[...] = (normed * second).astype(BF16).reshape(2, 4, PART, WIDTH)
    pl.semaphore_wait(barrier, len(partners))

    slices = group(arrived.at[pl.ds(0, 3)])
    for k in (1, 3, 2):
        for b in range(4):
            columns = columns_of((x + k) % 4, b)
            send(teach.at[:, :, columns], arrived.at[x, :, :, pl.ds(b * 256, 256)], device(dx=k), slices)
    head_z = group(head)
    send(head, heads.at[mine], device(dz=4), head_z)
    head_y = group(heads.at[pl.ds(0, 6)])
    for k in (1, 3, 2):
        send(head, heads.at[mine], device(dy=k), head_y)
    parts = group(extra_in)
    for k in (1, 3, 2):
        send(extra_out.at[:, (x + k) % 4], extra_in.at[k - 1], device(dx=k), parts)

    def rows_out(h):
        here = rows_b.at[h, :, x]
        into = group(rows_b.at[h, :, pl.ds(0, 2)])
        for k in (1, -1):
            send(here, here, device(dx=k), into)
        return into

    def rows_on(h, found):
        arrive(found)
        left, right = rows_b.at[h, pl.ds(0, 2), (x + 3) % 4], rows_b.at[h, pl.ds(2, 2), (x + 1) % 4]
        into = group(rows_b.at[h, :, 0])
        send(left, left, device(dx=1), into)
        send(right, right, device(dx=-1), into)
        return into

    def tails_out(h):
        tail = rows_b.at[h, x, 4]
        into = group(rows_b.at[h, pl.ds(0, 3), 4])
        for k in (1, 3, 2):
            send(tail, tail, device(dx=k), into)
        return into

    rows_a = rows_out(0)

    arrive(slices)
    for copy in owned:
        copy.wait()
    own = dot(permutation(128, image_order), arrived[...].astype(F32).reshape(128, SLICE).astype(BF16), ((1,), (0,)))
    target = (near_target, far_target)
    near_target[0, :, core] = own.astype(BF16).reshape(8, 16, SLICE)
    places = {0: (0, 0), -1: (0, 1), 1: (0, 2), -2: (0, 3), 4: (1, 0), -4: (1, 0), 3: (1, 1), -3: (1, 2), 2: (1, 3)}

    def chunk(step, half):
        h, q = places[step]
        return target[h].at[q, pl.ds(half * 4, 4), core]

    shared = [group(target[h].at[:, :, 0]) for h in range(2)]
    chunks_sent = used[1]
    used[1] += 1
    sent_views[chunks_sent] = near_target.at[:, pl.ds(0, 7)]

    def pass_on(step, half, ways):
        piece = chunk(step, half)
        found = [send(piece, chunk(step - way, half), device(dz=way), group(piece), chunks_sent) for way in ways]
        send(piece, piece, device(dc=1), shared[places[step][0]])
        return found[0] if found else None

    def first_step():
        up, down = [None, None], [None, None]
        for half in range(2):
            up[half] = send(chunk(0, half), chunk(-1, half), device(dz=1), group(chunk(0, half)), chunks_sent)
            other = 1 - half
            down[other] = send(chunk(0, other), chunk(1, other), device(dz=-1), group(chunk(0, other)), chunks_sent)
        for half in range(2):
            pass_on(0, half, ())
        return up, down

    from_low, from_high = first_step()

    def ring_step(step, halves=(0, 1)):
        last = step == 3
        for half in halves:
            from_low[half].wait_recv()
            from_low[half] = pass_on(-step, half, () if last and half == 1 else (1,))
            other = 1 - half
            from_high[other].wait_recv()
            from_high[other] = pass_on(step, other, () if last and other == 0 else (-1,))

    arrive(parts)
    quarter = extra_out[:, x].astype(F32)
    quarter += extra_in[0].astype(F32) + extra_in[1].astype(F32) + extra_in[2].astype(F32)
    rows_b[:, x, 4] = quarter.astype(BF16)
    tails_a = tails_out(0)
    rows_b1 = rows_out(1)

    arrive(head_z)
    theirs = heads.at[t * 2 + 1 - zh]
    for k in (1, 3, 2):
        send(theirs, theirs, device(dy=k), head_y)

    ring_step(1, (0,))
    rows_a = rows_on(0, rows_a)
    tails_b = tails_out(1)
    ring_step(1, (1,))
    ring_step(2, (0,))
    rows_b1 = rows_on(1, rows_b1)
    ring_step(2, (1,))
    arrive(head_y)
    arrive(rows_a)
    arrive(tails_a)

    extra_image = jnp.int32(0)
    extra_weight = jnp.float32(0)
    image, weights = [], []
    for b in range(4):
        count = used_slots[g, 0, b * 2 + zh]
        twice = count >= 2
        extra_image += jnp.where(twice, images[g, 0, 1, b * 2 + zh], 0)
        extra_weight += jnp.where(twice, 1.0, 0.0).astype(F32)
        image.append(images[g, 0, 0, b * 2 + zh])
        weights.append(jnp.where(count >= 1, 1.0, 0.0).astype(F32))
    image.append(extra_image)
    weights.append(extra_weight)
    row = lax.broadcasted_iota(jnp.int32, (1, GROUP), 1)
    slot_of = (row // PART) % 5
    weight = jnp.zeros((1, GROUP), F32)
    for i in range(5):
        weight = jnp.where(slot_of == i, weights[i], weight)
    here = (slot_of == x) | ((slot_of == 4) & (row // 160 == x))
    loss = jnp.float32(0)

    def targets(h, q):
        found = [target[h][q, image[i]].reshape(PART, SLICE) for i in range(5)]
        return jnp.concatenate(found, axis=0).astype(F32)

    def forward(h):
        def step(b, carry):
            rows = rows_b[h, pl.ds(b * 2, 2)].reshape(320, WIDTH)
            out = dot(rows, heads[...].reshape(SLICE, WIDTH), ((1,), (1,)))
            logits[h, pl.ds(b * 2, 2)] = out.reshape(2, 160, SLICE)
            return carry

        lax.fori_loop(0, 2, step, 0)

    lane = lax.broadcasted_iota(jnp.int32, (160, 128), 1)

    def statistics(h):
        def step(q, carry):
            lg = logits[h, q]
            tg = targets(h, q)
            inner = jnp.sum(lg * tg, axis=-1, keepdims=True)
            lsq = jnp.sum(lg * lg, axis=-1, keepdims=True)
            tsq = jnp.sum(tg * tg, axis=-1, keepdims=True)
            at = pl.ds(pl.multiple_of(q * 160, 32), 160)
            sums[h, at, :] = jnp.where(lane == 0, inner, jnp.where(lane == 1, lsq, tsq))
            return carry

        lax.fori_loop(0, 4, step, 0)
        for k in range(GROUP // 128):
            at = pl.ds(k * 128, 128)
            stat_out[h, :, at] = jnp.transpose(sums[h, at, :])[:4]
        into = group(stat_in.at[:, h])
        for k in (1, 3, 2):
            send(stat_out.at[h], stat_in.at[k - 1, h], device(dx=k), into)
        return into

    def factors(h):
        total = (stat_out[h] + stat_in[0, h] + stat_in[1, h] + stat_in[2, h]) * (1.0 / FEAT)
        inner, lsq, tsq = total[0:1], total[1:2], total[2:3]
        rl, rt = lax.rsqrt(lsq + 1e-06), lax.rsqrt(tsq + 1e-06)
        on_target = weight * rl * rt * (-1.0 / 16.0)
        on_logits = weight * inner * rt * rl * rl * rl * (1.0 / 16.0)
        pair = jnp.concatenate([on_target, on_logits, jnp.zeros((126, GROUP), F32)], axis=0)
        for k in range(GROUP // 128):
            cols[h, k * 128:(k + 1) * 128, :] = jnp.transpose(pair[:, k * 128:(k + 1) * 128])

        def step(q, carry):
            found = cols[h, pl.ds(pl.multiple_of(q * 160, 32), 160), :]
            dl = found[:, 0:1] * targets(h, q) + found[:, 1:2] * logits[h, q]
            dlogits[h, q] = dl.astype(BF16)
            return carry

        lax.fori_loop(0, 4, step, 0)
        return jnp.sum(jnp.where(here, weight * (1.0 - inner * rl * rt), 0.0)) * (1.0 / TOTAL)

    def row_gradient(h):
        def step(b, carry):
            part = dot(dlogits[h, pl.ds(b * 2, 2)].reshape(320, SLICE), heads[...].reshape(SLICE, WIDTH), ((1,), (0,)))
            part = part.reshape(2, 5, PART, WIDTH)
            d_all[h, pl.ds(b * 2, 2)] = part
            d_out[h, pl.ds(b * 2, 2)] = part.astype(BF16)
            return carry

        lax.fori_loop(0, 2, step, 0)

    def send_rows(h):
        low, high = pl.ds(0, 2), pl.ds(2, 2)
        across = (x + 2) % 4
        relay = group(relay_in.at[:, h])
        send(d_out.at[h, low, across], relay_in.at[0, h], device(dx=1), relay)
        send(d_out.at[h, high, across], relay_in.at[1, h], device(dx=-1), relay)
        return relay

    def send_extra(h):
        ext = group(e_in.at[:, h])
        for k in (1, 3, 2):
            send(d_out.at[h, (x + k) % 4, 4], e_in.at[k - 1, h], device(dx=k), ext)
        return ext

    def send_plain(h):
        low, high = pl.ds(0, 2), pl.ds(2, 2)
        main = group(d_in.at[:, h])
        send(d_out.at[h, high, (x + 1) % 4], d_in.at[0, h, high], device(dx=1), main)
        send(d_out.at[h, low, (x + 3) % 4], d_in.at[1, h, low], device(dx=-1), main)
        return main

    def relay_on(h, relay, main):
        low, high = pl.ds(0, 2), pl.ds(2, 2)
        after, before = (x + 1) % 4, (x + 3) % 4
        arrive(relay)
        relay_out[0, h] = (d_all[h, low, after] + relay_in[0, h].astype(F32)).astype(BF16)
        send(relay_out.at[0, h], d_in.at[0, h, low], device(dx=1), main)
        relay_out[1, h] = (d_all[h, high, before] + relay_in[1, h].astype(F32)).astype(BF16)
        send(relay_out.at[1, h], d_in.at[1, h, high], device(dx=-1), main)

    def extra_sum(h, ext):
        arrive(ext)
        total = d_all[h, x, 4]
        for k in range(3):
            total += e_in[k, h].astype(F32)
        e_all[h, x] = total.astype(BF16)
        piece = e_all.at[h, x]
        into = group(e_all.at[h, pl.ds(0, 3)])
        for k in (1, 3, 2):
            send(piece, piece, device(dx=k), into)
        return into

    forward(0)
    arrive(shared[0])
    stats_a = statistics(0)
    ring_step(3, (0,))
    arrive(rows_b1)
    arrive(tails_b)
    forward(1)
    ring_step(3, (1,))
    arrive(stats_a)
    loss += factors(0)
    from_low[0].wait_recv()
    pass_on(-4, 0, ())
    from_high[1].wait_recv()
    pass_on(4, 1, ())
    row_gradient(0)
    relay_a = send_rows(0)
    arrive(shared[1])
    stats_b = statistics(1)

    def head_part(h, columns):
        lhs = dlogits[h, :, :, columns].reshape(GROUP, 256)
        return dot(lhs, rows_b[h].reshape(GROUP, WIDTH), ((0,), (0,)))

    def columns_for(k):
        return pl.ds(pl.multiple_of((t + k) % 4 * 256, 256), 256)

    for k in (1, 3, 2, 0):
        g_near[k] = head_part(0, columns_for(k))
    ext_a = send_extra(0)
    main_a = send_plain(0)
    arrive(stats_b)
    loss += factors(1)

    far, close = (1 - zh) * 128, zh * 128
    gain_part = jnp.zeros((1, WIDTH), F32)
    away = [group(g_in.at[:, pl.ds(0, 64)]) for _ in range(2)]
    near = group(n_in)
    turned = group(y_relay)

    def send_half(k, start, size, into):
        at = pl.ds(pl.multiple_of(start, 64), size)
        send(g_out.at[k - 1, at], g_in.at[k - 1, at], device(dy=k), into)

    for k in (2, 1, 3, 0):
        to = (t + k) % 4
        part = g_near[k] + head_part(1, columns_for(k))
        weights = heads[pl.ds(to * 2, 2)].reshape(256, WIDTH).astype(F32)
        gain_part += jnp.sum(part * weights, axis=0, keepdims=True)
        if k:
            g_out[k - 1] = part.astype(BF16)
            send_half(k, far, 64, away[0])
            g_near[k] = part
        else:
            g_own[...] = part
        if k == 3:
            for other in (2, 1, 3):
                send_half(other, far + 64, 64, away[1])
            relay_on(0, relay_a, main_a)

    which = lax.broadcasted_iota(jnp.int32, (2, WIDTH), 0)
    tiny = jnp.where(which == 0, gain_part / gain[...], loss)
    tiny_out[0] = tiny
    tiny_x = group(tiny_in.at[pl.ds(0, 3)])
    for k in (1, 3, 2):
        send(tiny_out.at[0], tiny_in.at[k - 1], device(dx=k), tiny_x)
    row_gradient(1)
    relay_b = send_rows(1)
    ext_b = send_extra(1)
    main_b = send_plain(1)
    arrive(tiny_x)
    tiny += tiny_in[0] + tiny_in[1] + tiny_in[2]
    tiny_out[1] = tiny
    tiny_y = group(tiny_in.at[pl.ds(3, 3)])
    for k in (1, 3, 2):
        send(tiny_out.at[1], tiny_in.at[2 + k], device(dy=k), tiny_y)
    def rows_from_y(start, size):
        at = pl.ds(pl.multiple_of(start, 64), size)
        part = g_own[at, :]
        for k in range(3):
            part += g_in[k, at].astype(F32)
        return part

    relay_on(1, relay_b, main_b)
    ext_all = [extra_sum(0, ext_a)]
    across = []
    for c in range(2):
        arrive(away[c])
        at = pl.ds(c * 64, 64)
        gz_out[at, :] = rows_from_y(far + c * 64, 64).astype(BF16)
        across.append(group(gz_in.at[at]))
        send(gz_out.at[at], gz_in.at[at], device(dz=4), across[c])
        if c == 0:
            at = pl.ds(pl.multiple_of(close, 64), 64)
            send(g_out.at[1, at], y_relay.at[0], device(dy=1), turned)
            at = pl.ds(pl.multiple_of(close + 64, 64), 64)
            send(g_out.at[1, at], y_relay.at[1], device(dy=-1), turned)
            send(g_out.at[0, at], n_in.at[0, pl.ds(64, 64)], device(dy=1), near)
            at = pl.ds(pl.multiple_of(close, 64), 64)
            send(g_out.at[2, at], n_in.at[1, pl.ds(0, 64)], device(dy=-1), near)
    ext_all.append(extra_sum(1, ext_b))
    arrive(turned)
    at = pl.ds(pl.multiple_of(close, 64), 64)
    y_sum[0] = (g_near[1, at, :] + y_relay[0].astype(F32)).astype(BF16)
    send(y_sum.at[0], n_in.at[0, pl.ds(0, 64)], device(dy=1), near)
    at = pl.ds(pl.multiple_of(close + 64, 64), 64)
    y_sum[1] = (g_near[3, at, :] + y_relay[1].astype(F32)).astype(BF16)
    send(y_sum.at[1], n_in.at[1, pl.ds(64, 64)], device(dy=-1), near)
    arrive(tiny_y)
    tiny += tiny_in[3] + tiny_in[4] + tiny_in[5]
    tiny_out[2] = tiny
    tiny_z = group(tiny_in.at[6])
    send(tiny_out.at[2], tiny_in.at[6], device(dz=4), tiny_z)

    def finish(dnormed, part):
        dx = dnormed.reshape(MAIN, WIDTH) * gain[...]
        unit = xhat[part, :]
        drop = jnp.mean(dx, axis=-1, keepdims=True)
        along = jnp.mean(dx * unit, axis=-1, keepdims=True)
        out = (rstd[part, :][:, 0:1] * (dx - drop - unit * along)).astype(BF16)
        sgrad_o[part, :] = dot(order, out, ((0,), (0,))).astype(BF16)

    arrive(main_a)
    arrive(main_b)
    finish(d_all[:, :, x] + d_in[0].astype(F32) + d_in[1].astype(F32), pl.ds(0, MAIN))
    arrive(ext_all[0])
    arrive(ext_all[1])
    finish(e_all[...].astype(F32) * second, pl.ds(MAIN, MAIN))
    arrive(near)
    hgrad_o[...] = g_own[pl.ds(pl.multiple_of(close, 64), 128), :] + n_in[0].astype(F32) + n_in[1].astype(F32)
    arrive(across[0])
    arrive(across[1])
    hgrad_o[...] += gz_in[...].astype(F32)
    arrive(tiny_z)
    tiny += tiny_in[6]
    gain_o[...] = tiny[0:1]
    loss_o[0] = tiny[1, 0]
    assert used == [RECV_SEMS, SEND_SEMS], used
    for index, view in sent_views.items():
        pltpu.make_async_copy(view, view, send_sem.at[index]).wait()


def shards(teacher_feats, student_feats, norm_gain, head_weight, slot_image, slot_count):
    vmem = pl.BlockSpec(memory_space=pltpu.VMEM)
    smem = pl.BlockSpec(memory_space=pltpu.SMEM)
    anywhere = pl.BlockSpec(memory_space=pl.ANY)
    operands = (
        teacher_feats, student_feats.reshape(2 * MAIN, WIDTH), norm_gain, head_weight.reshape(128, WIDTH),
        slot_image.transpose(0, 1, 3, 2), slot_count,
    )
    loss, gain_grad, sgrad, hgrad = pl.pallas_call(
        kernel,
        out_shape=(
            jax.ShapeDtypeStruct((1,), F32),
            pltpu.VMEM((1, WIDTH), F32),
            pltpu.VMEM((2 * MAIN, WIDTH), BF16),
            pltpu.VMEM((128, WIDTH), F32),
        ),
        in_specs=[anywhere] * 6,
        out_specs=(smem, vmem, vmem, vmem),
        scratch_shapes=[
            pltpu.VMEM((4, 8, 4, SLICE), BF16),
            pltpu.VMEM((4, 8, 2, 16, SLICE), BF16),
            pltpu.VMEM((4, 8, 2, 16, SLICE), BF16),
            pltpu.VMEM((8, 128, WIDTH), BF16),
            pltpu.VMEM((2, 4, 5, PART, WIDTH), BF16),
            pltpu.VMEM((2, 4, PART, WIDTH), BF16),
            pltpu.VMEM((3, 2, PART, WIDTH), BF16),
            pltpu.VMEM((2 * MAIN, WIDTH), F32),
            pltpu.VMEM((2 * MAIN, 128), F32),
            pltpu.VMEM((2, 4, 160, SLICE), F32),
            pltpu.VMEM((2, 4, 160, SLICE), BF16),
            pltpu.VMEM((2, GROUP, 128), F32),
            pltpu.VMEM((2, GROUP, 128), F32),
            pltpu.VMEM((2, 4, GROUP), F32),
            pltpu.VMEM((3, 2, 4, GROUP), F32),
            pltpu.VMEM((3, 2, WIDTH), F32),
            pltpu.VMEM((7, 2, WIDTH), F32),
            pltpu.VMEM((4, 256, WIDTH), F32),
            pltpu.VMEM((3, 256, WIDTH), BF16),
            pltpu.VMEM((256, WIDTH), F32),
            pltpu.VMEM((3, 256, WIDTH), BF16),
            pltpu.VMEM((2, 64, WIDTH), BF16),
            pltpu.VMEM((2, 64, WIDTH), BF16),
            pltpu.VMEM((2, 128, WIDTH), BF16),
            pltpu.VMEM((128, WIDTH), BF16),
            pltpu.VMEM((128, WIDTH), BF16),
            pltpu.VMEM((2, 4, 5, PART, WIDTH), F32),
            pltpu.VMEM((2, 4, 5, PART, WIDTH), BF16),
            pltpu.VMEM((2, 2, 4, PART, WIDTH), BF16),
            pltpu.VMEM((2, 2, 2, PART, WIDTH), BF16),
            pltpu.VMEM((2, 2, 2, PART, WIDTH), BF16),
            pltpu.VMEM((3, 2, PART, WIDTH), BF16),
            pltpu.VMEM((2, 4, PART, WIDTH), BF16),
            pltpu.VMEM((2 * MAIN, WIDTH), BF16),
            pltpu.VMEM((1, WIDTH), F32),
            pltpu.SMEM((8, 1, 2, 8), jnp.int32),
            pltpu.SMEM((8, 1, 8), jnp.int32),
            pltpu.SemaphoreType.DMA((SEND_SEMS,)),
            pltpu.SemaphoreType.DMA((RECV_SEMS,)),
            pltpu.SemaphoreType.DMA((7,)),
        ],
        compiler_params=pltpu.CompilerParams(
            collective_id=0, has_side_effects=True, vmem_limit_bytes=44 << 20
        ),
        name="head_step",
    )(*[pltpu.with_memory_space_constraint(operand, pltpu.HBM) for operand in operands])
    return (
        loss,
        sgrad.reshape(student_feats.shape),
        hgrad.reshape(1, 128, WIDTH),
        gain_grad,
    )


def solution(mesh):
    return jax.shard_map(
        shards,
        mesh=mesh,
        in_specs=(
            P("teacher", ("group", "dp"), None),
            P("group", "teacher", "dp", None, None, None),
            P("group", None),
            P("group", ("teacher", "dp"), None),
            P(None, "teacher", None, None),
            P(None, "teacher", None),
        ),
        out_specs=(
            P("group"),
            P("group", "teacher", "dp", None, None, None),
            P("group", ("teacher", "dp"), None),
            P("group", None),
        ),
        check_vma=False,
    )
```

```python
import jax
import jax.numpy as jnp
from jax import lax
from jax.experimental import pallas as pl
from jax.experimental.pallas import tpu as pltpu
from jax.sharding import PartitionSpec as P

MESH = pl.DeviceIdType.MESH
F32 = jnp.float32
BF16 = jnp.bfloat16

FEAT = 4096
WIDTH = 768
PATCHES = 256
SLICE = 1024
MAIN = 256
PART = 32
GROUP = 640
TOTAL = 32 * PATCHES
RECV_SEMS, SEND_SEMS = 45, 32


def permutation(size, source_of):
    rows = lax.broadcasted_iota(jnp.int32, (size, size), 0)
    cols = lax.broadcasted_iota(jnp.int32, (size, size), 1)
    return jnp.where(source_of(rows) == cols, 1.0, 0.0).astype(BF16)


def image_order(n):
    return (n // 4 % 4) * 32 + (n // 16) * 4 + n % 4


def dot(a, b, dims):
    return lax.dot_general(a, b, (dims, ((), ())), preferred_element_type=F32)


def kernel(
    teach, feats, gain_h, head, images_h, used_slots_h,
    loss_o, gain_o, sgrad_o, hgrad_o,
    arrived, near_target, far_target, heads, rows_b, extra_out, extra_in,
    xhat, rstd, logits, dlogits, sums, cols,
    stat_out, stat_in, tiny_out, tiny_in, g_near,
    g_out, g_own, g_in, y_relay, y_sum, n_in, gz_out, gz_in,
    d_all, d_out, d_in, relay_out, relay_in, e_in, e_all,
    feats_v, gain, images, used_slots, send_sem, recv_sem, local_sem,
):
    t = lax.axis_index("teacher")
    g = lax.axis_index("group")
    d = lax.axis_index("dp")
    x, zh = d // 2, d % 2
    zl, core = g // 2, g % 2
    z = zh * 4 + zl

    def device(dx=0, dy=0, dz=0, dc=0):
        to_z = (z + dz + 8) % 8
        return {
            "teacher": (t + dy + 4) % 4,
            "group": (to_z % 4) * 2 + (core + dc) % 2,
            "dp": ((x + dx + 4) % 4) * 2 + to_z // 4,
        }

    used = [0, 0]

    def group(view):
        index = used[0]
        used[0] += 1
        return (index, view)

    def send(src, dst, to, into, sent=None):
        if sent is None:
            if into[0] not in sent_by:
                sent_by[into[0]] = used[1]
                sent_views[used[1]] = into[1]
                used[1] += 1
            sent = sent_by[into[0]]
        copy = pltpu.make_async_remote_copy(
            src_ref=src, dst_ref=dst, send_sem=send_sem.at[sent],
            recv_sem=recv_sem.at[into[0]], device_id=to, device_id_type=MESH,
        )
        copy.start()
        return copy

    sent_by, sent_views = {}, {}

    def arrive(into):
        pltpu.make_async_copy(into[1], into[1], recv_sem.at[into[0]]).wait()

    barrier = pltpu.get_barrier_semaphore()
    partners = [device(dx=k) for k in (1, 2, 3)] + [device(dy=k) for k in (1, 2, 3)]
    partners += [device(dz=k) for k in (1, -1, 4)] + [device(dc=1)]
    for to in partners:
        pl.semaphore_signal(barrier, inc=1, device_id=to, device_id_type=MESH)

    def patch_order(n):
        h, q, c, xs, p = n // 128, n // 32 % 4, n // 16 % 2, n // 4 % 4, n % 4
        away = jnp.where(q == 1, 7, jnp.where(q == 2, 1, jnp.where(q == 3, 6, 0)))
        at = (z + away + 4 * h) % 8
        return (at % 4) * 64 + c * 32 + xs * 8 + (at // 4) * 4 + p

    mine = t * 2 + zh
    inputs = [
        pltpu.make_async_copy(src, dst, local_sem.at[3 + n])
        for n, (src, dst) in enumerate(((images_h, images), (used_slots_h, used_slots), (gain_h, gain), (feats, feats_v)))
    ]
    for copy in inputs:
        copy.start()

    def columns_of(to, b):
        return pl.ds(pl.multiple_of(b * SLICE + to * 256, 256), 256)

    owned = [pltpu.make_async_copy(head, heads.at[mine], local_sem.at[1])]
    own_columns = [
        pltpu.make_async_copy(
            teach.at[:, columns_of(x, b)], arrived.at[x, :, pl.ds(b * 256, 256)], local_sem.at[2]
        )
        for b in range(4)
    ]
    for copy in own_columns:
        copy.start()
    owned.append(pltpu.make_async_copy(arrived.at[x], arrived.at[x], local_sem.at[2]))
    owned[0].start()
    for copy in inputs:
        copy.wait()
    second = jnp.where(used_slots[g, 0, d] >= 2, 1.0, 0.0).astype(F32)
    order = permutation(MAIN, patch_order)
    for slot in range(2):
        part = pl.ds(slot * MAIN, MAIN)
        values = dot(order, feats_v[part, :], ((1,), (0,)))
        center = values - jnp.mean(values, axis=-1, keepdims=True)
        rs = lax.rsqrt(jnp.mean(center * center, axis=-1, keepdims=True) + 1e-06)
        unit = center * rs
        xhat[part, :] = unit
        rstd[part, :] = jnp.broadcast_to(rs, (MAIN, 128))
        normed = unit * gain[...]
        if slot == 0:
            rows_b[:, :, x] = normed.astype(BF16).reshape(2, 4, PART, WIDTH)
        else:
            extra_out[...] = (normed * second).astype(BF16).reshape(2, 4, PART, WIDTH)
    pl.semaphore_wait(barrier, len(partners))

    slices = group(arrived.at[pl.ds(0, 3)])
    for k in (1, 3, 2):
        for b in range(4):
            columns = columns_of((x + k) % 4, b)
            send(teach.at[:, columns], arrived.at[x, :, pl.ds(b * 256, 256)], device(dx=k), slices)
    head_z = group(head)
    send(head, heads.at[mine], device(dz=4), head_z)
    head_y = group(heads.at[pl.ds(0, 6)])
    for k in (1, 3, 2):
        send(head, heads.at[mine], device(dy=k), head_y)
    parts = group(extra_in)
    for k in (1, 3, 2):
        send(extra_out.at[:, (x + k) % 4], extra_in.at[k - 1], device(dx=k), parts)

    def rows_out(h):
        here = rows_b.at[h, :, x]
        into = group(rows_b.at[h, :, pl.ds(0, 2)])
        for k in (1, -1):
            send(here, here, device(dx=k), into)
        return into

    def rows_on(h, found):
        arrive(found)
        left, right = rows_b.at[h, pl.ds(0, 2), (x + 3) % 4], rows_b.at[h, pl.ds(2, 2), (x + 1) % 4]
        into = group(rows_b.at[h, :, 0])
        send(left, left, device(dx=1), into)
        send(right, right, device(dx=-1), into)
        return into

    def tails_out(h):
        tail = rows_b.at[h, x, 4]
        into = group(rows_b.at[h, pl.ds(0, 3), 4])
        for k in (1, 3, 2):
            send(tail, tail, device(dx=k), into)
        return into

    rows_a = rows_out(0)

    arrive(slices)
    for copy in owned:
        copy.wait()
    own = dot(permutation(128, image_order), arrived[...].reshape(128, SLICE), ((1,), (0,)))
    target = (near_target, far_target)
    near_target[0, :, core] = own.astype(BF16).reshape(8, 16, SLICE)
    places = {0: (0, 0), -1: (0, 1), 1: (0, 2), -2: (0, 3), 4: (1, 0), -4: (1, 0), 3: (1, 1), -3: (1, 2), 2: (1, 3)}

    def chunk(step, half):
        h, q = places[step]
        return target[h].at[q, pl.ds(half * 4, 4), core]

    shared = [group(target[h].at[:, :, 0]) for h in range(2)]
    chunks_sent = used[1]
    used[1] += 1
    sent_views[chunks_sent] = near_target.at[:, pl.ds(0, 7)]

    def pass_on(step, half, ways):
        piece = chunk(step, half)
        found = [send(piece, chunk(step - way, half), device(dz=way), group(piece), chunks_sent) for way in ways]
        send(piece, piece, device(dc=1), shared[places[step][0]])
        return found[0] if found else None

    def first_step():
        up, down = [None, None], [None, None]
        for half in range(2):
            up[half] = send(chunk(0, half), chunk(-1, half), device(dz=1), group(chunk(0, half)), chunks_sent)
            other = 1 - half
            down[other] = send(chunk(0, other), chunk(1, other), device(dz=-1), group(chunk(0, other)), chunks_sent)
        for half in range(2):
            pass_on(0, half, ())
        return up, down

    from_low, from_high = first_step()

    def ring_step(step, halves=(0, 1)):
        last = step == 3
        for half in halves:
            from_low[half].wait_recv()
            from_low[half] = pass_on(-step, half, () if last and half == 1 else (1,))
            other = 1 - half
            from_high[other].wait_recv()
            from_high[other] = pass_on(step, other, () if last and other == 0 else (-1,))

    arrive(parts)
    quarter = extra_out[:, x].astype(F32)
    quarter += extra_in[0].astype(F32) + extra_in[1].astype(F32) + extra_in[2].astype(F32)
    rows_b[:, x, 4] = quarter.astype(BF16)
    tails_a = tails_out(0)
    rows_b1 = rows_out(1)

    arrive(head_z)
    theirs = heads.at[t * 2 + 1 - zh]
    for k in (1, 3, 2):
        send(theirs, theirs, device(dy=k), head_y)

    ring_step(1, (0,))
    rows_a = rows_on(0, rows_a)
    tails_b = tails_out(1)
    ring_step(1, (1,))
    ring_step(2, (0,))
    rows_b1 = rows_on(1, rows_b1)
    ring_step(2, (1,))
    arrive(head_y)
    arrive(rows_a)
    arrive(tails_a)

    extra_image = jnp.int32(0)
    extra_weight = jnp.float32(0)
    image, weights = [], []
    for b in range(4):
        count = used_slots[g, 0, b * 2 + zh]
        twice = count >= 2
        extra_image += jnp.where(twice, images[g, 0, 1, b * 2 + zh], 0)
        extra_weight += jnp.where(twice, 1.0, 0.0).astype(F32)
        image.append(images[g, 0, 0, b * 2 + zh])
        weights.append(jnp.where(count >= 1, 1.0, 0.0).astype(F32))
    image.append(extra_image)
    weights.append(extra_weight)
    row = lax.broadcasted_iota(jnp.int32, (1, GROUP), 1)
    slot_of = (row // PART) % 5
    weight = jnp.zeros((1, GROUP), F32)
    for i in range(5):
        weight = jnp.where(slot_of == i, weights[i], weight)
    here = (slot_of == x) | ((slot_of == 4) & (row // 160 == x))
    loss = jnp.float32(0)

    def targets(h, q):
        found = [target[h][q, image[i]].reshape(PART, SLICE) for i in range(5)]
        return jnp.concatenate(found, axis=0).astype(F32)

    def forward(h):
        def step(b, carry):
            rows = rows_b[h, pl.ds(b * 2, 2)].reshape(320, WIDTH)
            out = dot(rows, heads[...].reshape(SLICE, WIDTH), ((1,), (1,)))
            logits[h, pl.ds(b * 2, 2)] = out.reshape(2, 160, SLICE)
            return carry

        lax.fori_loop(0, 2, step, 0)

    lane = lax.broadcasted_iota(jnp.int32, (160, 128), 1)

    def statistics(h):
        def step(q, carry):
            lg = logits[h, q]
            tg = targets(h, q)
            inner = jnp.sum(lg * tg, axis=-1, keepdims=True)
            lsq = jnp.sum(lg * lg, axis=-1, keepdims=True)
            tsq = jnp.sum(tg * tg, axis=-1, keepdims=True)
            at = pl.ds(pl.multiple_of(q * 160, 32), 160)
            sums[h, at, :] = jnp.where(lane == 0, inner, jnp.where(lane == 1, lsq, tsq))
            return carry

        lax.fori_loop(0, 4, step, 0)
        for k in range(GROUP // 128):
            at = pl.ds(k * 128, 128)
            stat_out[h, :, at] = jnp.transpose(sums[h, at, :])[:4]
        into = group(stat_in.at[:, h])
        for k in (1, 3, 2):
            send(stat_out.at[h], stat_in.at[k - 1, h], device(dx=k), into)
        return into

    def factors(h):
        total = (stat_out[h] + stat_in[0, h] + stat_in[1, h] + stat_in[2, h]) * (1.0 / FEAT)
        inner, lsq, tsq = total[0:1], total[1:2], total[2:3]
        rl, rt = lax.rsqrt(lsq + 1e-06), lax.rsqrt(tsq + 1e-06)
        on_target = weight * rl * rt * (-1.0 / 16.0)
        on_logits = weight * inner * rt * rl * rl * rl * (1.0 / 16.0)
        pair = jnp.concatenate([on_target, on_logits, jnp.zeros((126, GROUP), F32)], axis=0)
        for k in range(GROUP // 128):
            cols[h, k * 128:(k + 1) * 128, :] = jnp.transpose(pair[:, k * 128:(k + 1) * 128])

        def step(q, carry):
            found = cols[h, pl.ds(pl.multiple_of(q * 160, 32), 160), :]
            dl = found[:, 0:1] * targets(h, q) + found[:, 1:2] * logits[h, q]
            dlogits[h, q] = dl.astype(BF16)
            return carry

        lax.fori_loop(0, 4, step, 0)
        return jnp.sum(jnp.where(here, weight * (1.0 - inner * rl * rt), 0.0)) * (1.0 / TOTAL)

    def row_gradient(h):
        def step(b, carry):
            part = dot(dlogits[h, pl.ds(b * 2, 2)].reshape(320, SLICE), heads[...].reshape(SLICE, WIDTH), ((1,), (0,)))
            part = part.reshape(2, 5, PART, WIDTH)
            d_all[h, pl.ds(b * 2, 2)] = part
            d_out[h, pl.ds(b * 2, 2)] = part.astype(BF16)
            return carry

        lax.fori_loop(0, 2, step, 0)

    def send_rows(h):
        low, high = pl.ds(0, 2), pl.ds(2, 2)
        across = (x + 2) % 4
        relay = group(relay_in.at[:, h])
        send(d_out.at[h, low, across], relay_in.at[0, h], device(dx=1), relay)
        send(d_out.at[h, high, across], relay_in.at[1, h], device(dx=-1), relay)
        return relay

    def send_extra(h):
        ext = group(e_in.at[:, h])
        for k in (1, 3, 2):
            send(d_out.at[h, (x + k) % 4, 4], e_in.at[k - 1, h], device(dx=k), ext)
        return ext

    def send_plain(h):
        low, high = pl.ds(0, 2), pl.ds(2, 2)
        main = group(d_in.at[:, h])
        send(d_out.at[h, high, (x + 1) % 4], d_in.at[0, h, high], device(dx=1), main)
        send(d_out.at[h, low, (x + 3) % 4], d_in.at[1, h, low], device(dx=-1), main)
        return main

    def relay_on(h, relay, main):
        low, high = pl.ds(0, 2), pl.ds(2, 2)
        after, before = (x + 1) % 4, (x + 3) % 4
        arrive(relay)
        relay_out[0, h] = (d_all[h, low, after] + relay_in[0, h].astype(F32)).astype(BF16)
        send(relay_out.at[0, h], d_in.at[0, h, low], device(dx=1), main)
        relay_out[1, h] = (d_all[h, high, before] + relay_in[1, h].astype(F32)).astype(BF16)
        send(relay_out.at[1, h], d_in.at[1, h, high], device(dx=-1), main)

    def extra_sum(h, ext):
        arrive(ext)
        total = d_all[h, x, 4]
        for k in range(3):
            total += e_in[k, h].astype(F32)
        e_all[h, x] = total.astype(BF16)
        piece = e_all.at[h, x]
        into = group(e_all.at[h, pl.ds(0, 3)])
        for k in (1, 3, 2):
            send(piece, piece, device(dx=k), into)
        return into

    forward(0)
    arrive(shared[0])
    stats_a = statistics(0)
    ring_step(3, (0,))
    arrive(rows_b1)
    arrive(tails_b)
    forward(1)
    ring_step(3, (1,))
    arrive(stats_a)
    loss += factors(0)
    from_low[0].wait_recv()
    pass_on(-4, 0, ())
    from_high[1].wait_recv()
    pass_on(4, 1, ())
    row_gradient(0)
    relay_a = send_rows(0)
    arrive(shared[1])
    stats_b = statistics(1)

    def head_part(h, columns):
        lhs = dlogits[h, :, :, columns].reshape(GROUP, 256)
        return dot(lhs, rows_b[h].reshape(GROUP, WIDTH), ((0,), (0,)))

    def columns_for(k):
        return pl.ds(pl.multiple_of((t + k) % 4 * 256, 256), 256)

    for k in (1, 3, 2, 0):
        g_near[k] = head_part(0, columns_for(k))
    ext_a = send_extra(0)
    main_a = send_plain(0)
    arrive(stats_b)
    loss += factors(1)

    far, close = (1 - zh) * 128, zh * 128
    gain_part = jnp.zeros((1, WIDTH), F32)
    away = [group(g_in.at[:, pl.ds(0, 64)]) for _ in range(2)]
    near = group(n_in)
    turned = group(y_relay)

    def send_half(k, start, size, into):
        at = pl.ds(pl.multiple_of(start, 64), size)
        send(g_out.at[k - 1, at], g_in.at[k - 1, at], device(dy=k), into)

    for k in (2, 1, 3, 0):
        to = (t + k) % 4
        part = g_near[k] + head_part(1, columns_for(k))
        weights = heads[pl.ds(to * 2, 2)].reshape(256, WIDTH).astype(F32)
        gain_part += jnp.sum(part * weights, axis=0, keepdims=True)
        if k:
            g_out[k - 1] = part.astype(BF16)
            send_half(k, far, 64, away[0])
            g_near[k] = part
        else:
            g_own[...] = part
        if k == 3:
            for other in (2, 1, 3):
                send_half(other, far + 64, 64, away[1])
            relay_on(0, relay_a, main_a)

    which = lax.broadcasted_iota(jnp.int32, (2, WIDTH), 0)
    tiny = jnp.where(which == 0, gain_part / gain[...], loss)
    tiny_out[0] = tiny
    tiny_x = group(tiny_in.at[pl.ds(0, 3)])
    for k in (1, 3, 2):
        send(tiny_out.at[0], tiny_in.at[k - 1], device(dx=k), tiny_x)
    row_gradient(1)
    relay_b = send_rows(1)
    ext_b = send_extra(1)
    main_b = send_plain(1)
    arrive(tiny_x)
    tiny += tiny_in[0] + tiny_in[1] + tiny_in[2]
    tiny_out[1] = tiny
    tiny_y = group(tiny_in.at[pl.ds(3, 3)])
    for k in (1, 3, 2):
        send(tiny_out.at[1], tiny_in.at[2 + k], device(dy=k), tiny_y)
    def rows_from_y(start, size):
        at = pl.ds(pl.multiple_of(start, 64), size)
        part = g_own[at, :]
        for k in range(3):
            part += g_in[k, at].astype(F32)
        return part

    relay_on(1, relay_b, main_b)
    ext_all = [extra_sum(0, ext_a)]
    across = []
    for c in range(2):
        arrive(away[c])
        at = pl.ds(c * 64, 64)
        gz_out[at, :] = rows_from_y(far + c * 64, 64).astype(BF16)
        across.append(group(gz_in.at[at]))
        send(gz_out.at[at], gz_in.at[at], device(dz=4), across[c])
        if c == 0:
            at = pl.ds(pl.multiple_of(close, 64), 64)
            send(g_out.at[1, at], y_relay.at[0], device(dy=1), turned)
            at = pl.ds(pl.multiple_of(close + 64, 64), 64)
            send(g_out.at[1, at], y_relay.at[1], device(dy=-1), turned)
            send(g_out.at[0, at], n_in.at[0, pl.ds(64, 64)], device(dy=1), near)
            at = pl.ds(pl.multiple_of(close, 64), 64)
            send(g_out.at[2, at], n_in.at[1, pl.ds(0, 64)], device(dy=-1), near)
    ext_all.append(extra_sum(1, ext_b))
    arrive(turned)
    at = pl.ds(pl.multiple_of(close, 64), 64)
    y_sum[0] = (g_near[1, at, :] + y_relay[0].astype(F32)).astype(BF16)
    send(y_sum.at[0], n_in.at[0, pl.ds(0, 64)], device(dy=1), near)
    at = pl.ds(pl.multiple_of(close + 64, 64), 64)
    y_sum[1] = (g_near[3, at, :] + y_relay[1].astype(F32)).astype(BF16)
    send(y_sum.at[1], n_in.at[1, pl.ds(64, 64)], device(dy=-1), near)
    arrive(tiny_y)
    tiny += tiny_in[3] + tiny_in[4] + tiny_in[5]
    tiny_out[2] = tiny
    tiny_z = group(tiny_in.at[6])
    send(tiny_out.at[2], tiny_in.at[6], device(dz=4), tiny_z)

    def finish(dnormed, part):
        dx = dnormed.reshape(MAIN, WIDTH) * gain[...]
        unit = xhat[part, :]
        drop = jnp.mean(dx, axis=-1, keepdims=True)
        along = jnp.mean(dx * unit, axis=-1, keepdims=True)
        out = (rstd[part, :][:, 0:1] * (dx - drop - unit * along)).astype(BF16)
        sgrad_o[part, :] = dot(order, out, ((0,), (0,))).astype(BF16)

    arrive(main_a)
    arrive(main_b)
    finish(d_all[:, :, x] + d_in[0].astype(F32) + d_in[1].astype(F32), pl.ds(0, MAIN))
    arrive(ext_all[0])
    arrive(ext_all[1])
    finish(e_all[...].astype(F32) * second, pl.ds(MAIN, MAIN))
    arrive(near)
    hgrad_o[...] = g_own[pl.ds(pl.multiple_of(close, 64), 128), :] + n_in[0].astype(F32) + n_in[1].astype(F32)
    arrive(across[0])
    arrive(across[1])
    hgrad_o[...] += gz_in[...].astype(F32)
    arrive(tiny_z)
    tiny += tiny_in[6]
    gain_o[...] = tiny[0:1]
    loss_o[0] = tiny[1, 0]
    assert used == [RECV_SEMS, SEND_SEMS], used
    for index, view in sent_views.items():
        pltpu.make_async_copy(view, view, send_sem.at[index]).wait()


def shards(teacher_feats, student_feats, norm_gain, head_weight, slot_image, slot_count):
    vmem = pl.BlockSpec(memory_space=pltpu.VMEM)
    smem = pl.BlockSpec(memory_space=pltpu.SMEM)
    anywhere = pl.BlockSpec(memory_space=pl.ANY)
    operands = (
        student_feats.reshape(2 * MAIN, WIDTH), norm_gain, head_weight.reshape(128, WIDTH),
        slot_image.transpose(0, 1, 3, 2), slot_count,
    )
    loss, gain_grad, sgrad, hgrad = pl.pallas_call(
        kernel,
        out_shape=(
            jax.ShapeDtypeStruct((1,), F32),
            pltpu.VMEM((1, WIDTH), F32),
            pltpu.VMEM((2 * MAIN, WIDTH), BF16),
            pltpu.VMEM((128, WIDTH), F32),
        ),
        in_specs=[anywhere] * 6,
        out_specs=(smem, vmem, vmem, vmem),
        scratch_shapes=[
            pltpu.VMEM((4, 32, SLICE), BF16),
            pltpu.VMEM((4, 8, 2, 16, SLICE), BF16),
            pltpu.VMEM((4, 8, 2, 16, SLICE), BF16),
            pltpu.VMEM((8, 128, WIDTH), BF16),
            pltpu.VMEM((2, 4, 5, PART, WIDTH), BF16),
            pltpu.VMEM((2, 4, PART, WIDTH), BF16),
            pltpu.VMEM((3, 2, PART, WIDTH), BF16),
            pltpu.VMEM((2 * MAIN, WIDTH), F32),
            pltpu.VMEM((2 * MAIN, 128), F32),
            pltpu.VMEM((2, 4, 160, SLICE), F32),
            pltpu.VMEM((2, 4, 160, SLICE), BF16),
            pltpu.VMEM((2, GROUP, 128), F32),
            pltpu.VMEM((2, GROUP, 128), F32),
            pltpu.VMEM((2, 4, GROUP), F32),
            pltpu.VMEM((3, 2, 4, GROUP), F32),
            pltpu.VMEM((3, 2, WIDTH), F32),
            pltpu.VMEM((7, 2, WIDTH), F32),
            pltpu.VMEM((4, 256, WIDTH), F32),
            pltpu.VMEM((3, 256, WIDTH), BF16),
            pltpu.VMEM((256, WIDTH), F32),
            pltpu.VMEM((3, 256, WIDTH), BF16),
            pltpu.VMEM((2, 64, WIDTH), BF16),
            pltpu.VMEM((2, 64, WIDTH), BF16),
            pltpu.VMEM((2, 128, WIDTH), BF16),
            pltpu.VMEM((128, WIDTH), BF16),
            pltpu.VMEM((128, WIDTH), BF16),
            pltpu.VMEM((2, 4, 5, PART, WIDTH), F32),
            pltpu.VMEM((2, 4, 5, PART, WIDTH), BF16),
            pltpu.VMEM((2, 2, 4, PART, WIDTH), BF16),
            pltpu.VMEM((2, 2, 2, PART, WIDTH), BF16),
            pltpu.VMEM((2, 2, 2, PART, WIDTH), BF16),
            pltpu.VMEM((3, 2, PART, WIDTH), BF16),
            pltpu.VMEM((2, 4, PART, WIDTH), BF16),
            pltpu.VMEM((2 * MAIN, WIDTH), BF16),
            pltpu.VMEM((1, WIDTH), F32),
            pltpu.SMEM((8, 1, 2, 8), jnp.int32),
            pltpu.SMEM((8, 1, 8), jnp.int32),
            pltpu.SemaphoreType.DMA((SEND_SEMS,)),
            pltpu.SemaphoreType.DMA((RECV_SEMS,)),
            pltpu.SemaphoreType.DMA((7,)),
        ],
        compiler_params=pltpu.CompilerParams(
            collective_id=0, has_side_effects=True, vmem_limit_bytes=44 << 20
        ),
        name="head_step",
    )(teacher_feats.reshape(32, FEAT), *[pltpu.with_memory_space_constraint(operand, pltpu.HBM) for operand in operands])
    return (
        loss,
        sgrad.reshape(student_feats.shape),
        hgrad.reshape(1, 128, WIDTH),
        gain_grad,
    )


def solution(mesh):
    return jax.shard_map(
        shards,
        mesh=mesh,
        in_specs=(
            P("teacher", ("group", "dp"), None),
            P("group", "teacher", "dp", None, None, None),
            P("group", None),
            P("group", ("teacher", "dp"), None),
            P(None, "teacher", None, None),
            P(None, "teacher", None),
        ),
        out_specs=(
            P("group"),
            P("group", "teacher", "dp", None, None, None),
            P("group", ("teacher", "dp"), None),
            P("group", None),
        ),
        check_vma=False,
    )
```
